32 devices in a mesh: dp: 8 (over y, x, core), pipe: 4 (over z).
Axes of the slice: x: 2, y: 2, z: 4, core: 2. Of those that a mesh axis runs over, the one named last changes fastest.
Arguments:
- latents_in: bfloat16 [3, 512, 3072], P(None, 'dp'), may hold values from -6 to 6
- context_cache: bfloat16 [2, 256, 3072], P(None, 'dp'), may hold values from -6 to 6
- w_qk: bfloat16 [4, 3072, 3072], P('pipe', 'dp'), may hold values from -2.75 to 2.75
- w_v: bfloat16 [4, 3072, 1536], P('pipe'), may hold values from -0.109375 to 0.109375
- w_out: bfloat16 [4, 3072, 1536], P('pipe'), may hold values from -0.15625 to 0.15625
- tile_mask: int32 [3, 8, 2], P(None, 'dp'), may hold values from 0 to 1, as said below
- out_cotangent: bfloat16 [4, 3, 512, 3072], P('pipe', None, 'dp'), may hold values from -6 to 6
Outputs:
- grad_out_proj: float32 [4, 3072, 1536], P('pipe', 'dp')
The draws below stay inside these ranges and needn't reach their ends.
Inputs may be any that keep to these rules, and one draw needn't show every extreme that they name: `tile_mask`: for the r-th tile of a block, key tile r + 1 is always allowed and key tiles above r + 1 never; key tile 0 is the 32 context rows.
All inputs are finite; a program needn't handle non-finite values.
Results may differ from the reference program's by a relative error of at most 0.018.
Values may be sent and summed in bfloat16 or wider, within the bound.
A program may use at most 128 MiB of HBM per device.

```python
import jax
import jax.numpy as jnp
from jax import lax

D = 3072
HEADS = 12
HDIM = 128
TILE = 64
TOK_DEV = 64
MB = 3
LAG = 2
SECTIONS = 4
CTX = 32
HD = 1536
TOKENS = 512
CTX_ALL = 256
QTILES = 8
KTILES = 2
N_DP = 8


def draw_w_qk(key, part):
    key = jax.random.fold_in(key, 13)
    first_key, second_key = jax.random.split(key, 2)
    factor = D ** (-0.5)
    query_part = jnp.clip(jax.random.normal(first_key, (SECTIONS, D, HEADS, HDIM), jnp.float32), -6.0, 6.0) * factor
    other_part = jnp.clip(jax.random.normal(second_key, (SECTIONS, D, HEADS, HDIM), jnp.float32), -6.0, 6.0) * factor
    key_part = other_part
    joined = jnp.concatenate([query_part.reshape(SECTIONS, D, HEADS * HDIM), key_part.reshape(SECTIONS, D, HEADS * HDIM)], axis=2)
    joined = jnp.clip(joined, -2.75, 2.75)
    return joined.astype(jnp.bfloat16)


def draw_tile_mask(key, part):
    key = jax.random.fold_in(key, 7)
    first_key, second_key = jax.random.split(key)
    per_block = TOK_DEV // TILE
    block_count = QTILES // per_block
    levels = jax.random.randint(first_key, (MB, block_count, 1, 1), 1, 5)
    levels = jnp.broadcast_to(levels, (MB, block_count, per_block, 1)).reshape(MB, QTILES, 1)
    random_bits = jax.random.randint(second_key, (MB, QTILES, KTILES), 0, 4)
    row_tile = (jnp.arange(QTILES, dtype=jnp.int32) % per_block)[:, None]
    column = jnp.arange(KTILES, dtype=jnp.int32)[None, :]
    earlier = (random_bits < levels).astype(jnp.int32)
    pattern = jnp.where(column == row_tile + 1, 1, jnp.where(column > row_tile + 1, 0, earlier))
    return pattern.astype(jnp.int32)


def spiked(drawn, own_key, source, target, blocks, factor):
    owner, partner = [(jnp.arange(drawn.shape[axis_at]) // (drawn.shape[axis_at] // blocks)).reshape([-1 if axis == axis_at else 1 for axis in range(drawn.ndim)]) for axis_at in (source, target)]
    chosen = jax.random.permutation(own_key, blocks)[partner]
    strong = (owner == chosen) | (owner == (partner + blocks // 2) % blocks)
    return jnp.where(strong, factor * drawn, drawn)


def steps_of(stream_key, shape, shards, smallest, high):
    factor_of = 1.0
    for position, shards_of in shards:
        steps = jax.random.uniform(jax.random.fold_in(jax.random.fold_in(stream_key, 6), position), (shards_of,), jnp.float32, smallest / len(shards), high / len(shards))
        factor_of = factor_of * jnp.repeat(jnp.exp(steps), shape[position] // shards_of).reshape((-1,) + (1,) * (len(shape) - 1 - position))
    return factor_of


def gaussian(stream_key, dims, scale, bound, cuts=(), held_as=jnp.bfloat16):
    entries = scale * jax.random.normal(stream_key, dims, jnp.float32)
    if cuts:
        entries = entries * steps_of(stream_key, dims, cuts, -0.22, 0.18)
    return jnp.clip(entries, -bound, bound).astype(held_as)


def noise_with(rng, shape, deviation, most, shards, heavy, kind=jnp.bfloat16):
    values = deviation * jax.random.normal(rng, shape, jnp.float32)
    if shards:
        values = values * steps_of(rng, shape, shards, -0.22, 0.18)
    return jnp.clip(spiked(values, jax.random.fold_in(rng, 3), *heavy), -most, most).astype(kind)


def setup_inputs(seed: int = 0) -> dict:
    arg_keys = jax.random.split(jax.random.key(seed), 8)
    return {
        "latents_in": gaussian(arg_keys[0], (MB, TOKENS, D), 1.0, 6.0, ((1, 8),)),
        "context_cache": gaussian(arg_keys[1], (LAG, CTX_ALL, D), 1.0, 6.0, ((1, 8),)),
        "w_qk": draw_w_qk(jax.random.fold_in(arg_keys[7], 71), 0),
        "w_v": gaussian(arg_keys[3], (SECTIONS, D, HD), D ** -0.5, 0.109375, ((0, 4),)),
        "w_out": gaussian(arg_keys[4], (SECTIONS, D, HD), HD ** -0.5, 0.15625, ((0, 4),)),
        "tile_mask": draw_tile_mask(jax.random.fold_in(arg_keys[7], 71), 0),
        "out_cotangent": noise_with(arg_keys[6], (SECTIONS, MB, TOKENS, D), 1.0, 6.0, ((0, 4), (2, 8)), (2, 3, 8, 2.0)),
    }


def allowed_keys(tile_block):
    columns = jnp.concatenate([jnp.repeat(tile_block[:, :1], CTX, axis=1), jnp.repeat(tile_block[:, 1:], TILE, axis=1)], axis=1)
    return jnp.repeat(columns, TILE, axis=0) == 1

def section_step(hidden, context, tile_block, weights_qk, weights_v, weights_out):
    joined = jnp.concatenate([context, hidden], axis=0).astype(jnp.float32)
    normed = (joined * lax.rsqrt(lax.optimization_barrier(jnp.mean(joined * joined, axis=-1, keepdims=True)) + 1e-06)).astype(jnp.bfloat16)
    queries = jnp.dot(normed[CTX:], weights_qk[:, :HD], preferred_element_type=jnp.float32).astype(jnp.bfloat16)
    key_rows = jnp.dot(normed, weights_qk[:, HD:], preferred_element_type=jnp.float32).astype(jnp.bfloat16)
    value_rows = jnp.dot(normed, weights_v, preferred_element_type=jnp.float32).astype(jnp.bfloat16)
    query_heads = queries.reshape(TOK_DEV, HEADS, HDIM).astype(jnp.float32)
    key_heads = key_rows.reshape(CTX + TOK_DEV, HEADS, HDIM).astype(jnp.float32)
    value_heads = value_rows.reshape(CTX + TOK_DEV, HEADS, HDIM).astype(jnp.float32)
    scores = jnp.einsum('qhd,khd->hqk', query_heads, key_heads) * HDIM ** (-0.5)
    allowed = allowed_keys(tile_block)
    scores = jnp.where(allowed[None], scores, -1e+30)
    largest = lax.optimization_barrier(jnp.max(scores, axis=-1, keepdims=True))
    exponent = jnp.exp(scores - largest)
    attention = (exponent / lax.optimization_barrier(jnp.sum(exponent, axis=-1, keepdims=True))).astype(jnp.bfloat16)
    mixed_heads = jnp.einsum('hqk,khd->qhd', attention.astype(jnp.float32), value_heads)
    mixed_heads = mixed_heads.astype(jnp.bfloat16).reshape(TOK_DEV, HD)
    update = jnp.dot(mixed_heads, weights_out.T, preferred_element_type=jnp.float32)
    result = (hidden.astype(jnp.float32) + update).astype(jnp.bfloat16)
    return (result, mixed_heads)

def reference(latents_in, context_cache, w_qk, w_v, w_out, tile_mask, out_cotangent):
    blocks = N_DP
    latents = latents_in.reshape(MB, blocks, TOK_DEV, D)
    cached = context_cache.reshape(LAG, blocks, CTX, D)
    tile_masks = tile_mask.reshape(MB, blocks, TOK_DEV // TILE, KTILES)
    stepper = jax.vmap(section_step, in_axes=(0, 0, 0, None, None, None))
    finals = []
    mixed_list = [[] for section in range(SECTIONS)]
    for batch_index in range(MB):
        if batch_index < LAG:
            context = cached[batch_index]
        else:
            context = finals[batch_index - LAG][:, TOK_DEV - CTX:, :]
        hidden = latents[batch_index]
        for section in range(SECTIONS):
            hidden, mixed_heads = stepper(hidden, context, tile_masks[batch_index], w_qk[section], w_v[section], w_out[section])
            mixed_list[section].append(mixed_heads)
        finals.append(hidden)

    def accumulate(running, block_pair):
        partial_value = jnp.dot(block_pair[0].T, block_pair[1], preferred_element_type=jnp.float32).astype(jnp.bfloat16)
        partial_value = lax.optimization_barrier(partial_value)
        return (running + partial_value.astype(jnp.float32), None)
    gradients = []
    for section in range(SECTIONS):
        cotangent_rows = out_cotangent[section].reshape(MB, blocks, TOK_DEV, D).transpose(1, 0, 2, 3).reshape(blocks, MB * TOK_DEV, D)
        mixed_all = jnp.stack(mixed_list[section]).transpose(1, 0, 2, 3).reshape(blocks, MB * TOK_DEV, HD)
        running, unused = lax.scan(accumulate, jnp.zeros((D, HD), jnp.float32), (cotangent_rows, mixed_all))
        gradients.append(running)
    return jnp.stack(gradients)
```

```python
import functools

import jax
import jax.numpy as jnp
import numpy as np
from jax import lax
from jax.experimental import pallas as pl
from jax.experimental.pallas import tpu as pltpu
from jax.sharding import PartitionSpec as P

HEADS = 12
HDIM = 128
TILE = 64
MB = 3
LAG = 2
CHUNKS = 4
MESH = pl.DeviceIdType.MESH


def passed_along(block, axis, distance):
    devices = range(lax.axis_size(axis))
    route = [((i - distance) % len(devices), i) for i in devices]
    return lax.ppermute(block, axis, route)


def allowed_keys(tile_block, ctx_rows):
    columns = jnp.concatenate(
        [
            jnp.repeat(tile_block[:, :1], ctx_rows, axis=1),
            jnp.repeat(tile_block[:, 1:], TILE, axis=1),
        ],
        axis=1,
    )
    return jnp.repeat(columns, TILE, axis=0) == 1


def attend(hidden, context, tile_block, weights_q, weights_k, weights_v, weights_out):
    ctx_rows = context.shape[0]
    tok_rows = hidden.shape[0]
    heads_width = weights_v.shape[1]
    joined = jnp.concatenate([context, hidden], axis=0).astype(jnp.float32)
    normed = (joined * lax.rsqrt(jnp.mean(joined * joined, axis=-1, keepdims=True) + 1e-06)).astype(
        jnp.bfloat16
    )
    queries = jnp.dot(normed[ctx_rows:], weights_q, preferred_element_type=jnp.float32).astype(
        jnp.bfloat16
    )
    key_rows = jnp.dot(normed, weights_k, preferred_element_type=jnp.float32).astype(jnp.bfloat16)
    value_rows = jnp.dot(normed, weights_v, preferred_element_type=jnp.float32).astype(jnp.bfloat16)
    query_heads = queries.reshape(tok_rows, HEADS, HDIM)
    key_heads = key_rows.reshape(ctx_rows + tok_rows, HEADS, HDIM)
    value_heads = value_rows.reshape(ctx_rows + tok_rows, HEADS, HDIM)
    scores = jnp.einsum(
        "qhd,khd->hqk", query_heads, key_heads, preferred_element_type=jnp.float32
    ) * HDIM ** (-0.5)
    allowed = allowed_keys(tile_block, ctx_rows)
    scores = jnp.where(allowed[None], scores, -1e30)
    largest = jnp.max(scores, axis=-1, keepdims=True)
    exponent = jnp.exp(scores - largest)
    attention = (exponent / jnp.sum(exponent, axis=-1, keepdims=True)).astype(jnp.bfloat16)
    mixed_heads = jnp.einsum(
        "hqk,khd->qhd", attention, value_heads, preferred_element_type=jnp.float32
    )
    mixed_heads = mixed_heads.astype(jnp.bfloat16).reshape(tok_rows, heads_width)
    update = lax.dot_general(
        mixed_heads, weights_out, (((1,), (1,)), ((), ())), preferred_element_type=jnp.float32
    )
    result = (hidden.astype(jnp.float32) + update).astype(jnp.bfloat16)
    return (result, mixed_heads)


def local(latents_in, context_cache, w_qk, w_v, w_out, tile_mask, out_cotangent):
    segments = lax.axis_size("pipe")
    segment_index = lax.axis_index("pipe")
    tok_rows = latents_in.shape[1]
    model_width = latents_in.shape[2]
    ctx_rows = context_cache.shape[1]
    heads_width = w_v.shape[2]
    weights_q, weights_k = (
        lax.all_gather(w_qk[0][:, :heads_width], "dp", axis=0, tiled=True),
        lax.all_gather(w_qk[0][:, heads_width:], "dp", axis=0, tiled=True),
    )
    weights_v = w_v[0]
    weights_out = w_out[0]
    cotangent_local = out_cotangent[0]
    starts = [microbatch // LAG * segments + microbatch % LAG for microbatch in range(MB)]
    moments = starts[-1] + segments
    plan_table = np.full((moments, segments), -1, np.int32)
    for microbatch in range(MB):
        for section in range(segments):
            plan_table[starts[microbatch] + section, section] = microbatch
    roster = jnp.asarray(plan_table)
    records = jnp.zeros((MB, tok_rows, heads_width), jnp.bfloat16)
    incoming = jnp.zeros((tok_rows, model_width), jnp.bfloat16)
    incoming_ctx = jnp.zeros((ctx_rows, model_width), jnp.bfloat16)
    leading = segment_index == 0

    def advance(operands):
        hidden, context, chosen, kept = operands
        result, mixed_heads = attend(
            hidden, context, tile_mask[chosen], weights_q, weights_k, weights_v, weights_out
        )
        return (result, lax.dynamic_update_slice_in_dim(kept, mixed_heads[None], chosen, 0))

    def standby(operands):
        return (operands[0], operands[3])

    for moment in range(moments):
        current = roster[moment, segment_index]
        chosen = jnp.maximum(current, 0)
        hidden = jnp.where(leading, latents_in[chosen], incoming)
        first_context = jnp.where(
            chosen < LAG,
            context_cache[jnp.minimum(chosen, LAG - 1)],
            incoming[tok_rows - ctx_rows :],
        )
        context = jnp.where(leading, first_context, incoming_ctx)
        result, records = lax.cond(
            current >= 0, advance, standby, (hidden, context, chosen, records)
        )
        if moment + 1 < moments:
            incoming, incoming_ctx = passed_along((result, context), "pipe", 1)
    cotangent_rows = cotangent_local.reshape(MB * tok_rows, model_width)
    mixed_rows = records.reshape(MB * tok_rows, heads_width)
    gradient = lax.psum_scatter(
        lax.dot_general(
            cotangent_rows, mixed_rows, (((0,), (0,)), ((), ())), preferred_element_type=jnp.float32
        ).astype(jnp.bfloat16),
        "dp",
        scatter_dimension=0,
        tiled=True,
    ).astype(jnp.float32)
    return gradient[None]


def chip_neighbours(dp):
    core = dp % 2
    x = (dp // 2) % 2
    y = dp // 4
    sibling = dp + 1 - 2 * core
    along_x = y * 4 + (1 - x) * 2 + core
    along_y = (1 - y) * 4 + x * 2 + core
    across = (1 - y) * 4 + (1 - x) * 2 + core
    return sibling, along_x, along_y, across


def dot_nn(a, b):
    return jnp.dot(a, b, preferred_element_type=jnp.float32)


def dot_nt(a, b):
    return lax.dot_general(a, b, (((1,), (1,)), ((), ())), preferred_element_type=jnp.float32)


def dot_tn(a, b):
    return lax.dot_general(a, b, (((0,), (0,)), ((), ())), preferred_element_type=jnp.float32)


def row_scale(rows):
    wide = rows.astype(jnp.float32)
    return lax.rsqrt(jnp.mean(wide * wide, axis=-1, keepdims=True) + 1e-06)


def fused(
    n_dp, n_pipe, latents, cache, w_qk, w_v, w_out, bias, cot, out,
    wq, wk, wv, wo, given, hid, outgo, ctx2, qacc, kacc, vacc, qb, kb, vb, o_all, ct_all,
    ld_sem, w_send, w_recv, h_send, h_recv, c_send, c_recv, o_send, o_recv, t_send, t_recv,
):
    dp = lax.axis_index("dp")
    stage = lax.axis_index("pipe")
    sibling, along_x, along_y, across = chip_neighbours(dp)
    tok = latents.shape[1]
    ctx = cache.shape[1]
    width = latents.shape[2]
    heads_width = w_v.shape[1]
    shard = w_qk.shape[0]
    step = width // CHUNKS
    last = n_pipe - 1
    base = LAG * ctx

    loads = [
        pltpu.make_async_copy(cache.at[m], given.at[pl.ds(m * ctx, ctx)], ld_sem.at[m])
        for m in range(LAG)
    ]
    loads += [
        pltpu.make_async_copy(latents.at[m], given.at[pl.ds(base + m * tok, tok)], ld_sem.at[LAG + m])
        for m in range(MB)
    ]
    load_v = pltpu.make_async_copy(w_v, wv, ld_sem.at[LAG + MB])
    load_o = pltpu.make_async_copy(w_out, wo, ld_sem.at[LAG + MB + 1])
    own_rows = pl.ds(pl.multiple_of(dp * shard, shard), shard)
    own_q = pltpu.make_async_copy(
        w_qk.at[:, pl.ds(0, heads_width)], wq.at[own_rows], ld_sem.at[LAG + MB + 2]
    )
    own_k = pltpu.make_async_copy(
        w_qk.at[:, pl.ds(heads_width, heads_width)], wk.at[own_rows], ld_sem.at[LAG + MB + 3]
    )
    own_t = pltpu.make_async_copy(
        cot.at[:, :, pl.ds(pl.multiple_of(dp * shard, shard), shard)],
        ct_all.at[:, dp],
        ld_sem.at[LAG + MB + 4],
    )
    for copy in loads:
        copy.start()
    load_v.start()

    barrier = pltpu.get_barrier_semaphore()
    for k in range(1, n_dp):
        pl.semaphore_signal(barrier, 1, device_id=((dp + k) % n_dp, stage), device_id_type=MESH)
    for k in range(1, n_pipe):
        pl.semaphore_signal(barrier, 1, device_id=(dp, (stage + k) % n_pipe), device_id_type=MESH)
    pl.semaphore_wait(barrier, n_dp - 1 + n_pipe - 1)

    halves = (wq, wk)
    sent = []

    def rows_of(j):
        return pl.ds(pl.multiple_of(j * shard, shard), shard)

    def send_own(half, target):
        copy = pltpu.make_async_remote_copy(
            src_ref=w_qk.at[:, pl.ds(half * heads_width, heads_width)],
            dst_ref=halves[half].at[own_rows],
            send_sem=w_send.at[len(sent)],
            recv_sem=w_recv.at[dp, half],
            device_id=(target, stage),
            device_id_type=MESH,
        )
        copy.start()
        sent.append(copy)

    def piece(j, half, target, slot):
        ref = halves[half].at[rows_of(j)]
        return pltpu.make_async_remote_copy(
            src_ref=ref,
            dst_ref=ref,
            send_sem=w_send.at[slot],
            recv_sem=w_recv.at[j, half],
            device_id=(target, stage),
            device_id_type=MESH,
        )

    def forward(j, half, target):
        copy = piece(j, half, target, len(sent))
        copy.start()
        sent.append(copy)

    def arrived(j, half):
        piece(j, half, sibling, 0).wait_recv()

    send_own(0, along_y)
    send_own(1, along_x)
    send_own(1, along_y)
    send_own(0, along_x)
    send_own(0, sibling)
    send_own(1, sibling)
    own_q.start()
    own_k.start()
    load_o.start()
    own_t.start()

    for copy in loads:
        copy.wait()
    load_v.wait()
    tile = heads_width // 6

    @pl.loop(0, 6)
    def _(n):
        cols = pl.ds(pl.multiple_of(n * tile, tile), tile)
        vacc[:, cols] = dot_nn(given[...], wv[:, cols])

    qacc[...] = jnp.zeros_like(qacc)
    kacc[...] = jnp.zeros_like(kacc)

    @pl.when(stage == 0)
    def _():
        for m in range(MB):
            hid[m] = given[base + m * tok : base + (m + 1) * tok]

    wide = heads_width // 3

    def use(j, half):
        acc = (qacc, kacc)[half]
        weights = halves[half]
        first = base if half == 0 else 0

        @pl.loop(0, 3)
        def _(n):
            cols = pl.ds(pl.multiple_of(n * wide, wide), wide)
            acc[first:, cols] += dot_nn(given[first:, rows_of(j)], weights[rows_of(j), cols])

    own_q.wait()
    use(dp, 0)
    own_k.wait()
    use(dp, 1)
    arrived(sibling, 0)
    use(sibling, 0)
    arrived(sibling, 1)
    use(sibling, 1)
    arrived(along_y, 0)
    forward(along_y, 0, along_x)
    forward(along_y, 0, sibling)
    arrived(along_x, 1)
    forward(along_x, 1, along_y)
    forward(along_x, 1, sibling)
    use(along_y, 0)
    use(along_x, 1)
    arrived(along_y, 1)
    forward(along_y, 1, sibling)
    arrived(along_x, 0)
    forward(along_x, 0, sibling)
    use(along_y, 1)
    use(along_x, 0)
    sib_x, sib_y, sib_d = [
        neighbour + 1 - 2 * (dp % 2) for neighbour in (along_x, along_y, across)
    ]
    for j in (sib_y, sib_x):
        for half in range(2):
            arrived(j, half)
            use(j, half)
    for half in range(2):
        arrived(across, half)
        forward(across, half, sibling)
    for half in range(2):
        use(across, half)
    for half in range(2):
        arrived(sib_d, half)
        use(sib_d, half)

    cot_sent = []
    own_t.wait()
    for k in range(1, n_dp):
        target = (dp + k) % n_dp
        copy = pltpu.make_async_remote_copy(
            src_ref=cot.at[:, :, pl.ds(pl.multiple_of(target * shard, shard), shard)],
            dst_ref=ct_all.at[:, dp],
            send_sem=t_send.at[k],
            recv_sem=t_recv.at[dp],
            device_id=(target, stage),
            device_id_type=MESH,
        )
        copy.start()
        cot_sent.append(copy)

    load_o.wait()
    scale = row_scale(given[0:base])
    for m in range(LAG):
        rows = slice(m * ctx, (m + 1) * ctx)
        kb[m, 0:ctx] = (kacc[rows] * scale[rows]).astype(jnp.bfloat16)
        vb[m, 0:ctx] = (vacc[rows] * scale[rows]).astype(jnp.bfloat16)

    def hop(m, c, target):
        cols = pl.ds(c * step, step)
        return pltpu.make_async_remote_copy(
            src_ref=outgo.at[m, :, cols],
            dst_ref=hid.at[m, :, cols],
            send_sem=h_send.at[m, c],
            recv_sem=h_recv.at[m, c],
            device_id=(dp, target),
            device_id_type=MESH,
        )

    def loop_back(c, target, slot):
        ref = ctx2.at[:, pl.ds(c * step, step)]
        return pltpu.make_async_remote_copy(
            src_ref=ref,
            dst_ref=ref,
            send_sem=c_send.at[slot, c],
            recv_sem=c_recv.at[c],
            device_id=(dp, target),
            device_id_type=MESH,
        )

    def spread(m, k):
        target = (dp + k) % n_dp
        ref = o_all.at[m, dp]
        return pltpu.make_async_remote_copy(
            src_ref=ref,
            dst_ref=ref,
            send_sem=o_send.at[m, k],
            recv_sem=o_recv.at[m, dp],
            device_id=(target, stage),
            device_id_type=MESH,
        )

    def contract(rows, lhs, c, pairs):
        for acc, weights in pairs:
            @pl.loop(0, 3)
            def _(n):
                cols = pl.ds(pl.multiple_of(n * wide, wide), wide)
                term = dot_nn(lhs, weights[c * step : (c + 1) * step, cols])
                if c == 0:
                    acc[rows, cols] = term
                else:
                    acc[rows, cols] += term

    def process(m):
        rows = slice(base + m * tok, base + (m + 1) * tok)
        if m >= LAG:
            for c in range(CHUNKS):
                @pl.when(stage != last)
                def _():
                    loop_back(c, last, 0).wait_recv()

                contract(
                    slice(0, ctx), ctx2[:, c * step : (c + 1) * step], c, ((kacc, wk), (vacc, wv))
                )
            scale = row_scale(ctx2[...])
            kb[m, 0:ctx] = (kacc[0:ctx] * scale).astype(jnp.bfloat16)
            vb[m, 0:ctx] = (vacc[0:ctx] * scale).astype(jnp.bfloat16)

        @pl.when(stage > 0)
        def _():
            for c in range(CHUNKS):
                hop(m, c, (stage + 1) % n_pipe).wait_recv()
                contract(
                    rows,
                    hid[m, :, c * step : (c + 1) * step],
                    c,
                    ((qacc, wq), (kacc, wk), (vacc, wv)),
                )

        scale = row_scale(hid[m])
        qb[...] = (qacc[rows] * scale).astype(jnp.bfloat16)
        kb[m, ctx:] = (kacc[rows] * scale).astype(jnp.bfloat16)
        vb[m, ctx:] = (vacc[rows] * scale).astype(jnp.bfloat16)
        heads = [slice(h * HDIM, (h + 1) * HDIM) for h in range(HEADS)]
        scores = jnp.concatenate([dot_nt(qb[:, s], kb[m, :, s]) for s in heads], axis=0)
        scores = scores * HDIM ** (-0.5) + bias[m : m + 1, :]
        largest = jnp.max(scores, axis=-1, keepdims=True)
        exponent = jnp.exp(scores - largest)
        attention = (exponent / jnp.sum(exponent, axis=-1, keepdims=True)).astype(jnp.bfloat16)
        for h, s in enumerate(heads):
            o_all[m, dp, :, s] = dot_nn(
                attention[h * tok : (h + 1) * tok], vb[m, :, s]
            ).astype(jnp.bfloat16)
        if m == MB - 1:
            for k in range(1, n_dp):
                spread(m, k).start()

        @pl.when(stage != last)
        def _():
            for c in range(CHUNKS):
                cols = slice(c * step, (c + 1) * step)
                outgo[m, :, cols] = (
                    hid[m, :, cols].astype(jnp.float32) + dot_nt(o_all[m, dp], wo[cols, :])
                ).astype(jnp.bfloat16)
                hop(m, c, (stage + 1) % n_pipe).start()

        if m + LAG < MB:
            @pl.when(stage == last)
            def _():
                for c in range(CHUNKS):
                    cols = slice(c * step, (c + 1) * step)
                    ctx2[:, cols] = (
                        hid[m, tok - ctx :, cols].astype(jnp.float32)
                        + dot_nt(o_all[m, dp, tok - ctx :, :], wo[cols, :])
                    ).astype(jnp.bfloat16)
                    loop_back(c, 0, 0).start()
                for target in range(1, n_pipe - 1):
                    for c in range(CHUNKS):
                        loop_back(c, target, target).start()

        if m < MB - 1:
            for k in range(1, n_dp):
                spread(m, k).start()

    def gradient(m):
        if m == 0:
            for k in range(1, n_dp):
                source = (dp + k) % n_dp
                pltpu.make_async_remote_copy(
                    src_ref=ct_all.at[:, source],
                    dst_ref=ct_all.at[:, source],
                    send_sem=t_send.at[k],
                    recv_sem=t_recv.at[source],
                    device_id=(source, stage),
                    device_id_type=MESH,
                ).wait_recv()
        for k in range(1, n_dp):
            source = (dp + k) % n_dp
            pltpu.make_async_remote_copy(
                src_ref=o_all.at[m, source],
                dst_ref=o_all.at[m, source],
                send_sem=o_send.at[m, k],
                recv_sem=o_recv.at[m, source],
                device_id=(source, stage),
                device_id_type=MESH,
            ).wait_recv()

        left = ct_all[m].reshape(n_dp * tok, shard)

        @pl.loop(0, 3)
        def _(n):
            cols = pl.ds(pl.multiple_of(n * wide, wide), wide)
            term = dot_tn(left, o_all[m, :, :, cols].reshape(n_dp * tok, wide))
            if m == 0:
                out[:, cols] = term
            else:
                out[:, cols] += term

    for m in range(MB - 1):
        process(m)
    for m in range(MB - 1):
        gradient(m)
    process(MB - 1)
    gradient(MB - 1)

    for copy in sent + cot_sent:
        copy.wait_send()
    for m in range(MB):
        for k in range(1, n_dp):
            spread(m, k).wait_send()

    @pl.when(stage != last)
    def _():
        for m in range(MB):
            for c in range(CHUNKS):
                hop(m, c, (stage + 1) % n_pipe).wait_send()

    @pl.when(stage == last)
    def _():
        for target in range(n_pipe - 1):
            for c in range(CHUNKS):
                loop_back(c, target, target).wait_send()


def local_fused(latents_in, context_cache, w_qk, w_v, w_out, tile_mask, out_cotangent):
    n_dp = lax.axis_size("dp")
    n_pipe = lax.axis_size("pipe")
    tok, width = latents_in.shape[1:]
    ctx = context_cache.shape[1]
    heads_width = w_v.shape[2]
    shard = w_qk.shape[1]
    allowed = jnp.concatenate(
        [jnp.repeat(tile_mask[:, 0, :1], ctx, axis=1), jnp.repeat(tile_mask[:, 0, 1:], tok, axis=1)],
        axis=1,
    )
    bias = jnp.where(allowed == 1, 0.0, -1e30).astype(jnp.float32)
    rows = LAG * ctx + MB * tok
    keys = ctx + tok
    bf, f32 = jnp.bfloat16, jnp.float32
    dma = pltpu.SemaphoreType.DMA
    anywhere = pl.BlockSpec(memory_space=pl.ANY)
    vmem = pl.BlockSpec(memory_space=pltpu.VMEM)
    out = pl.pallas_call(
        functools.partial(fused, n_dp, n_pipe),
        out_shape=jax.ShapeDtypeStruct((shard, heads_width), f32),
        in_specs=[anywhere] * 5 + [vmem, anywhere],
        out_specs=vmem,
        scratch_shapes=[
            pltpu.VMEM((width, heads_width), bf),
            pltpu.VMEM((width, heads_width), bf),
            pltpu.VMEM((width, heads_width), bf),
            pltpu.VMEM((width, heads_width), bf),
            pltpu.VMEM((rows, width), bf),
            pltpu.VMEM((MB, tok, width), bf),
            pltpu.VMEM((MB, tok, width), bf),
            pltpu.VMEM((ctx, width), bf),
            pltpu.VMEM((rows, heads_width), f32),
            pltpu.VMEM((rows, heads_width), f32),
            pltpu.VMEM((rows, heads_width), f32),
            pltpu.VMEM((tok, heads_width), bf),
            pltpu.VMEM((MB, keys, heads_width), bf),
            pltpu.VMEM((MB, keys, heads_width), bf),
            pltpu.VMEM((MB, n_dp, tok, heads_width), bf),
            pltpu.VMEM((MB, n_dp, tok, shard), bf),
            dma((LAG + MB + 5,)),
            dma((14,)),
            dma((n_dp, 2)),
            dma((MB, CHUNKS)),
            dma((MB, CHUNKS)),
            dma((n_pipe - 1, CHUNKS)),
            dma((CHUNKS,)),
            dma((MB, n_dp)),
            dma((MB, n_dp)),
            dma((n_dp,)),
            dma((n_dp,)),
        ],
        compiler_params=pltpu.CompilerParams(
            collective_id=0, has_side_effects=True, vmem_limit_bytes=62 * 2**20
        ),
    )(latents_in, context_cache, w_qk[0], w_v[0], w_out[0], bias, out_cotangent[0])
    return out[None]


def solution(mesh):
    in_specs = (
        P(None, "dp", None),
        P(None, "dp", None),
        P("pipe", "dp", None),
        P("pipe", None, None),
        P("pipe", None, None),
        P(None, "dp", None),
        P("pipe", None, "dp", None),
    )
    out_specs = P("pipe", "dp", None)
    fits = mesh.shape["dp"] == 8 and mesh.shape["pipe"] > 1
    body = local_fused if fits else local
    return jax.shard_map(body, mesh=mesh, in_specs=in_specs, out_specs=out_specs, check_vma=False)
```

```python
import functools

import jax
import jax.numpy as jnp
import numpy as np
from jax import lax
from jax.experimental import pallas as pl
from jax.experimental.pallas import tpu as pltpu
from jax.sharding import PartitionSpec as P

HEADS = 12
HDIM = 128
TILE = 64
MB = 3
LAG = 2
PARTS = (1, 2, 3, 3, 2, 1)
CHUNKS = len(PARTS)
MESH = pl.DeviceIdType.MESH


def passed_along(block, axis, distance):
    devices = range(lax.axis_size(axis))
    route = [((i - distance) % len(devices), i) for i in devices]
    return lax.ppermute(block, axis, route)


def allowed_keys(tile_block, ctx_rows):
    columns = jnp.concatenate(
        [
            jnp.repeat(tile_block[:, :1], ctx_rows, axis=1),
            jnp.repeat(tile_block[:, 1:], TILE, axis=1),
        ],
        axis=1,
    )
    return jnp.repeat(columns, TILE, axis=0) == 1


def attend(hidden, context, tile_block, weights_q, weights_k, weights_v, weights_out):
    ctx_rows = context.shape[0]
    tok_rows = hidden.shape[0]
    heads_width = weights_v.shape[1]
    joined = jnp.concatenate([context, hidden], axis=0).astype(jnp.float32)
    normed = (joined * lax.rsqrt(jnp.mean(joined * joined, axis=-1, keepdims=True) + 1e-06)).astype(
        jnp.bfloat16
    )
    queries = jnp.dot(normed[ctx_rows:], weights_q, preferred_element_type=jnp.float32).astype(
        jnp.bfloat16
    )
    key_rows = jnp.dot(normed, weights_k, preferred_element_type=jnp.float32).astype(jnp.bfloat16)
    value_rows = jnp.dot(normed, weights_v, preferred_element_type=jnp.float32).astype(jnp.bfloat16)
    query_heads = queries.reshape(tok_rows, HEADS, HDIM)
    key_heads = key_rows.reshape(ctx_rows + tok_rows, HEADS, HDIM)
    value_heads = value_rows.reshape(ctx_rows + tok_rows, HEADS, HDIM)
    scores = jnp.einsum(
        "qhd,khd->hqk", query_heads, key_heads, preferred_element_type=jnp.float32
    ) * HDIM ** (-0.5)
    allowed = allowed_keys(tile_block, ctx_rows)
    scores = jnp.where(allowed[None], scores, -1e30)
    largest = jnp.max(scores, axis=-1, keepdims=True)
    exponent = jnp.exp(scores - largest)
    attention = (exponent / jnp.sum(exponent, axis=-1, keepdims=True)).astype(jnp.bfloat16)
    mixed_heads = jnp.einsum(
        "hqk,khd->qhd", attention, value_heads, preferred_element_type=jnp.float32
    )
    mixed_heads = mixed_heads.astype(jnp.bfloat16).reshape(tok_rows, heads_width)
    update = lax.dot_general(
        mixed_heads, weights_out, (((1,), (1,)), ((), ())), preferred_element_type=jnp.float32
    )
    result = (hidden.astype(jnp.float32) + update).astype(jnp.bfloat16)
    return (result, mixed_heads)


def local(latents_in, context_cache, w_qk, w_v, w_out, tile_mask, out_cotangent):
    segments = lax.axis_size("pipe")
    segment_index = lax.axis_index("pipe")
    tok_rows = latents_in.shape[1]
    model_width = latents_in.shape[2]
    ctx_rows = context_cache.shape[1]
    heads_width = w_v.shape[2]
    weights_q, weights_k = (
        lax.all_gather(w_qk[0][:, :heads_width], "dp", axis=0, tiled=True),
        lax.all_gather(w_qk[0][:, heads_width:], "dp", axis=0, tiled=True),
    )
    weights_v = w_v[0]
    weights_out = w_out[0]
    cotangent_local = out_cotangent[0]
    starts = [microbatch // LAG * segments + microbatch % LAG for microbatch in range(MB)]
    moments = starts[-1] + segments
    plan_table = np.full((moments, segments), -1, np.int32)
    for microbatch in range(MB):
        for section in range(segments):
            plan_table[starts[microbatch] + section, section] = microbatch
    roster = jnp.asarray(plan_table)
    records = jnp.zeros((MB, tok_rows, heads_width), jnp.bfloat16)
    incoming = jnp.zeros((tok_rows, model_width), jnp.bfloat16)
    incoming_ctx = jnp.zeros((ctx_rows, model_width), jnp.bfloat16)
    leading = segment_index == 0

    def advance(operands):
        hidden, context, chosen, kept = operands
        result, mixed_heads = attend(
            hidden, context, tile_mask[chosen], weights_q, weights_k, weights_v, weights_out
        )
        return (result, lax.dynamic_update_slice_in_dim(kept, mixed_heads[None], chosen, 0))

    def standby(operands):
        return (operands[0], operands[3])

    for moment in range(moments):
        current = roster[moment, segment_index]
        chosen = jnp.maximum(current, 0)
        hidden = jnp.where(leading, latents_in[chosen], incoming)
        first_context = jnp.where(
            chosen < LAG,
            context_cache[jnp.minimum(chosen, LAG - 1)],
            incoming[tok_rows - ctx_rows :],
        )
        context = jnp.where(leading, first_context, incoming_ctx)
        result, records = lax.cond(
            current >= 0, advance, standby, (hidden, context, chosen, records)
        )
        if moment + 1 < moments:
            incoming, incoming_ctx = passed_along((result, context), "pipe", 1)
    cotangent_rows = cotangent_local.reshape(MB * tok_rows, model_width)
    mixed_rows = records.reshape(MB * tok_rows, heads_width)
    gradient = lax.psum_scatter(
        lax.dot_general(
            cotangent_rows, mixed_rows, (((0,), (0,)), ((), ())), preferred_element_type=jnp.float32
        ).astype(jnp.bfloat16),
        "dp",
        scatter_dimension=0,
        tiled=True,
    ).astype(jnp.float32)
    return gradient[None]


def chip_neighbours(dp):
    core = dp % 2
    x = (dp // 2) % 2
    y = dp // 4
    sibling = dp + 1 - 2 * core
    along_x = y * 4 + (1 - x) * 2 + core
    along_y = (1 - y) * 4 + x * 2 + core
    across = (1 - y) * 4 + (1 - x) * 2 + core
    return sibling, along_x, along_y, across


def dot_nn(a, b):
    return jnp.dot(a, b, preferred_element_type=jnp.float32)


def dot_nt(a, b):
    return lax.dot_general(a, b, (((1,), (1,)), ((), ())), preferred_element_type=jnp.float32)


def dot_tn(a, b):
    return lax.dot_general(a, b, (((0,), (0,)), ((), ())), preferred_element_type=jnp.float32)


def row_scale(rows):
    wide = rows.astype(jnp.float32)
    return lax.rsqrt(jnp.mean(wide * wide, axis=-1, keepdims=True) + 1e-06)


def fused(
    n_dp, n_pipe, latents, cache, w_qk, w_v, w_out, bias, cot, out,
    wq, wk, wv, wo, given, hid, outgo, ctx2, qacc, kacc, vacc, qb, kb, vb, o_all, ct_all,
    ld_sem, w_send, w_recv, h_send, h_recv, c_send, c_recv, o_send, o_recv, t_send, t_recv, e_send, e_recv,
):
    dp = lax.axis_index("dp")
    stage = lax.axis_index("pipe")
    sibling, along_x, along_y, across = chip_neighbours(dp)
    tok = latents.shape[1]
    ctx = cache.shape[1]
    width = latents.shape[2]
    heads_width = w_v.shape[1]
    shard = w_qk.shape[0]
    unit = width // sum(PARTS)
    edges = [unit * sum(PARTS[:c]) for c in range(CHUNKS + 1)]
    last = n_pipe - 1
    base = LAG * ctx

    loads = [
        pltpu.make_async_copy(cache.at[m], given.at[pl.ds(m * ctx, ctx)], ld_sem.at[m])
        for m in range(LAG)
    ]
    loads += [
        pltpu.make_async_copy(latents.at[m], given.at[pl.ds(base + m * tok, tok)], ld_sem.at[LAG + m])
        for m in range(MB)
    ]
    load_v = pltpu.make_async_copy(w_v, wv, ld_sem.at[LAG + MB])
    load_o = pltpu.make_async_copy(w_out, wo, ld_sem.at[LAG + MB + 1])
    own_rows = pl.ds(pl.multiple_of(dp * shard, shard), shard)
    own_q = pltpu.make_async_copy(
        w_qk.at[:, pl.ds(0, heads_width)], wq.at[own_rows], ld_sem.at[LAG + MB + 2]
    )
    own_k = pltpu.make_async_copy(
        w_qk.at[:, pl.ds(heads_width, heads_width)], wk.at[own_rows], ld_sem.at[LAG + MB + 3]
    )
    own_t = pltpu.make_async_copy(
        cot.at[:, :, pl.ds(pl.multiple_of(dp * shard, shard), shard)],
        ct_all.at[:, dp],
        ld_sem.at[LAG + MB + 4],
    )
    for copy in loads:
        copy.start()
    load_v.start()

    barrier = pltpu.get_barrier_semaphore()
    for k in range(1, n_dp):
        pl.semaphore_signal(barrier, 1, device_id=((dp + k) % n_dp, stage), device_id_type=MESH)
    for k in range(1, n_pipe):
        pl.semaphore_signal(barrier, 1, device_id=(dp, (stage + k) % n_pipe), device_id_type=MESH)
    pl.semaphore_wait(barrier, n_dp - 1 + n_pipe - 1)

    halves = (wq, wk)
    sent = []

    def rows_of(j):
        return pl.ds(pl.multiple_of(j * shard, shard), shard)

    def send_own(half, target):
        copy = pltpu.make_async_remote_copy(
            src_ref=w_qk.at[:, pl.ds(half * heads_width, heads_width)],
            dst_ref=halves[half].at[own_rows],
            send_sem=w_send.at[len(sent)],
            recv_sem=w_recv.at[dp, half],
            device_id=(target, stage),
            device_id_type=MESH,
        )
        copy.start()
        sent.append(copy)

    def piece(j, half, target, slot):
        ref = halves[half].at[rows_of(j)]
        return pltpu.make_async_remote_copy(
            src_ref=ref,
            dst_ref=ref,
            send_sem=w_send.at[slot],
            recv_sem=w_recv.at[j, half],
            device_id=(target, stage),
            device_id_type=MESH,
        )

    def forward(j, half, target):
        copy = piece(j, half, target, len(sent))
        copy.start()
        sent.append(copy)

    def arrived(j, half):
        piece(j, half, sibling, 0).wait_recv()

    send_own(0, along_y)
    send_own(1, along_x)
    send_own(1, along_y)
    send_own(0, along_x)
    send_own(0, sibling)
    send_own(1, sibling)
    own_q.start()
    own_k.start()
    load_o.start()
    own_t.start()

    for copy in loads:
        copy.wait()
    load_v.wait()
    tile = heads_width // 6

    @pl.loop(0, 6)
    def _(n):
        cols = pl.ds(pl.multiple_of(n * tile, tile), tile)
        vacc[:, cols] = dot_nn(given[...], wv[:, cols])

    qacc[...] = jnp.zeros_like(qacc)
    kacc[...] = jnp.zeros_like(kacc)

    @pl.when(stage == 0)
    def _():
        for m in range(MB):
            hid[m] = given[base + m * tok : base + (m + 1) * tok]

    wide = heads_width // 3

    def use(j, half):
        acc = (qacc, kacc)[half]
        weights = halves[half]
        first = base if half == 0 else 0

        @pl.loop(0, 3)
        def _(n):
            cols = pl.ds(pl.multiple_of(n * wide, wide), wide)
            acc[first:, cols] += dot_nn(given[first:, rows_of(j)], weights[rows_of(j), cols])

    own_q.wait()
    use(dp, 0)
    own_k.wait()
    use(dp, 1)
    arrived(sibling, 0)
    use(sibling, 0)
    arrived(sibling, 1)
    use(sibling, 1)
    arrived(along_y, 0)
    forward(along_y, 0, along_x)
    forward(along_y, 0, sibling)
    arrived(along_x, 1)
    forward(along_x, 1, along_y)
    forward(along_x, 1, sibling)
    use(along_y, 0)
    use(along_x, 1)
    arrived(along_y, 1)
    forward(along_y, 1, sibling)
    arrived(along_x, 0)
    forward(along_x, 0, sibling)
    use(along_y, 1)
    use(along_x, 0)
    sib_x, sib_y, sib_d = [
        neighbour + 1 - 2 * (dp % 2) for neighbour in (along_x, along_y, across)
    ]
    for j in (sib_y, sib_x):
        for half in range(2):
            arrived(j, half)
            use(j, half)
    for half in range(2):
        arrived(across, half)
        forward(across, half, sibling)
    for half in range(2):
        use(across, half)
    for half in range(2):
        arrived(sib_d, half)
        use(sib_d, half)

    load_o.wait()
    scale = row_scale(given[0:base])
    for m in range(LAG):
        rows = slice(m * ctx, (m + 1) * ctx)
        kb[m, 0:ctx] = (kacc[rows] * scale[rows]).astype(jnp.bfloat16)
        vb[m, 0:ctx] = (vacc[rows] * scale[rows]).astype(jnp.bfloat16)

    def hop(m, c, target):
        cols = pl.ds(edges[c], edges[c + 1] - edges[c])
        return pltpu.make_async_remote_copy(
            src_ref=outgo.at[m, :, cols],
            dst_ref=hid.at[m, :, cols],
            send_sem=h_send.at[m, c],
            recv_sem=h_recv.at[m, c],
            device_id=(dp, target),
            device_id_type=MESH,
        )

    def loop_back(c, target, slot):
        ref = ctx2.at[:, pl.ds(edges[c], edges[c + 1] - edges[c])]
        return pltpu.make_async_remote_copy(
            src_ref=ref,
            dst_ref=ref,
            send_sem=c_send.at[slot, c],
            recv_sem=c_recv.at[c],
            device_id=(dp, target),
            device_id_type=MESH,
        )

    def spread(m, k):
        target = (dp + k) % n_dp
        ref = o_all.at[m, dp]
        return pltpu.make_async_remote_copy(
            src_ref=ref,
            dst_ref=ref,
            send_sem=o_send.at[m, k],
            recv_sem=o_recv.at[m, dp],
            device_id=(target, stage),
            device_id_type=MESH,
        )

    tail_sent = []

    def tail_piece(j, half, target, slot):
        ref = o_all.at[MB - 1, j, :, pl.ds(half * (heads_width // 2), heads_width // 2)]
        return pltpu.make_async_remote_copy(
            src_ref=ref,
            dst_ref=ref,
            send_sem=e_send.at[slot],
            recv_sem=e_recv.at[j, half],
            device_id=(target, stage),
            device_id_type=MESH,
        )

    def tail_send(j, half, target):
        copy = tail_piece(j, half, target, len(tail_sent))
        copy.start()
        tail_sent.append(copy)

    def tail_arrived(j, half):
        tail_piece(j, half, sibling, 0).wait_recv()

    def finish_exchange():
        tail_arrived(along_y, 0)
        tail_send(along_y, 0, along_x)
        tail_arrived(along_x, 1)
        tail_send(along_x, 1, along_y)
        tail_send(along_y, 0, sibling)
        tail_send(along_x, 1, sibling)
        tail_arrived(along_y, 1)
        tail_send(along_y, 1, sibling)
        tail_arrived(along_x, 0)
        tail_send(along_x, 0, sibling)
        for half in range(2):
            tail_arrived(across, half)
            tail_send(across, half, sibling)
        for j in (sibling, sib_y, sib_x, sib_d):
            for half in range(2):
                tail_arrived(j, half)

    def contract(rows, lhs, c, pairs):
        for acc, weights in pairs:
            term = dot_nn(lhs, weights[edges[c] : edges[c + 1], :])
            if c == 0:
                acc[rows] = term
            else:
                acc[rows] += term

    def process(m):
        rows = slice(base + m * tok, base + (m + 1) * tok)
        if m >= LAG:
            for c in range(CHUNKS):
                @pl.when(stage != last)
                def _():
                    loop_back(c, last, 0).wait_recv()

                contract(
                    slice(0, ctx), ctx2[:, edges[c] : edges[c + 1]], c, ((kacc, wk), (vacc, wv))
                )
            scale = row_scale(ctx2[...])
            kb[m, 0:ctx] = (kacc[0:ctx] * scale).astype(jnp.bfloat16)
            vb[m, 0:ctx] = (vacc[0:ctx] * scale).astype(jnp.bfloat16)

        @pl.when(stage > 0)
        def _():
            for c in range(CHUNKS):
                hop(m, c, (stage + 1) % n_pipe).wait_recv()
                contract(
                    rows,
                    hid[m, :, edges[c] : edges[c + 1]],
                    c,
                    ((qacc, wq), (kacc, wk), (vacc, wv)),
                )

        scale = row_scale(hid[m])
        qb[...] = (qacc[rows] * scale).astype(jnp.bfloat16)
        kb[m, ctx:] = (kacc[rows] * scale).astype(jnp.bfloat16)
        vb[m, ctx:] = (vacc[rows] * scale).astype(jnp.bfloat16)
        heads = [slice(h * HDIM, (h + 1) * HDIM) for h in range(HEADS)]
        scores = jnp.concatenate([dot_nt(qb[:, s], kb[m, :, s]) for s in heads], axis=0)
        scores = scores * HDIM ** (-0.5) + bias[m : m + 1, :]
        largest = jnp.max(scores, axis=-1, keepdims=True)
        exponent = jnp.exp(scores - largest)
        attention = (exponent / jnp.sum(exponent, axis=-1, keepdims=True)).astype(jnp.bfloat16)
        for h, s in enumerate(heads):
            o_all[m, dp, :, s] = dot_nn(
                attention[h * tok : (h + 1) * tok], vb[m, :, s]
            ).astype(jnp.bfloat16)
        if m == MB - 1:
            for half, target in ((0, along_y), (1, along_x), (1, along_y), (0, along_x)):
                tail_send(dp, half, target)
            for half in range(2):
                tail_send(dp, half, sibling)

        @pl.when(stage != last)
        def _():
            for c in range(CHUNKS):
                cols = slice(edges[c], edges[c + 1])
                outgo[m, :, cols] = (
                    hid[m, :, cols].astype(jnp.float32) + dot_nt(o_all[m, dp], wo[cols, :])
                ).astype(jnp.bfloat16)
                hop(m, c, (stage + 1) % n_pipe).start()

        if m + LAG < MB:
            @pl.when(stage == last)
            def _():
                for c in range(CHUNKS):
                    cols = slice(edges[c], edges[c + 1])
                    ctx2[:, cols] = (
                        hid[m, tok - ctx :, cols].astype(jnp.float32)
                        + dot_nt(o_all[m, dp, tok - ctx :, :], wo[cols, :])
                    ).astype(jnp.bfloat16)
                    loop_back(c, 0, 0).start()
                for c in range(CHUNKS):
                    loop_back(c, 0, 0).wait_send()
                for target in range(1, n_pipe - 1):
                    for c in range(CHUNKS):
                        loop_back(c, target, target).start()

        if m < MB - 1:
            for k in range(1, n_dp):
                spread(m, k).start()

    def gradient(m):
        if m == 0:
            for k in range(1, n_dp):
                source = (dp + k) % n_dp
                pltpu.make_async_remote_copy(
                    src_ref=ct_all.at[:, source],
                    dst_ref=ct_all.at[:, source],
                    send_sem=t_send.at[k],
                    recv_sem=t_recv.at[source],
                    device_id=(source, stage),
                    device_id_type=MESH,
                ).wait_recv()
        if m == MB - 1:
            finish_exchange()
        else:
            for k in range(1, n_dp):
                source = (dp + k) % n_dp
                pltpu.make_async_remote_copy(
                    src_ref=o_all.at[m, source],
                    dst_ref=o_all.at[m, source],
                    send_sem=o_send.at[m, k],
                    recv_sem=o_recv.at[m, source],
                    device_id=(source, stage),
                    device_id_type=MESH,
                ).wait_recv()

        left = ct_all[m].reshape(n_dp * tok, shard)

        @pl.loop(0, 3)
        def _(n):
            cols = pl.ds(pl.multiple_of(n * wide, wide), wide)
            term = dot_tn(left, o_all[m, :, :, cols].reshape(n_dp * tok, wide))
            if m == 0:
                out[:, cols] = term
            else:
                out[:, cols] += term

    process(0)
    cot_sent = []
    own_t.wait()
    for k in range(1, n_dp):
        target = (dp + k) % n_dp
        copy = pltpu.make_async_remote_copy(
            src_ref=cot.at[:, :, pl.ds(pl.multiple_of(target * shard, shard), shard)],
            dst_ref=ct_all.at[:, dp],
            send_sem=t_send.at[k],
            recv_sem=t_recv.at[dp],
            device_id=(target, stage),
            device_id_type=MESH,
        )
        copy.start()
        cot_sent.append(copy)
    for m in range(1, MB - 1):
        process(m)
    for m in range(MB - 1):
        gradient(m)
    process(MB - 1)
    gradient(MB - 1)

    for copy in sent + cot_sent + tail_sent:
        copy.wait_send()
    for m in range(MB - 1):
        for k in range(1, n_dp):
            spread(m, k).wait_send()

    @pl.when(stage != last)
    def _():
        for m in range(MB):
            for c in range(CHUNKS):
                hop(m, c, (stage + 1) % n_pipe).wait_send()

    @pl.when(stage == last)
    def _():
        for target in range(1, n_pipe - 1):
            for c in range(CHUNKS):
                loop_back(c, target, target).wait_send()


def local_fused(latents_in, context_cache, w_qk, w_v, w_out, tile_mask, out_cotangent):
    n_dp = lax.axis_size("dp")
    n_pipe = lax.axis_size("pipe")
    tok, width = latents_in.shape[1:]
    ctx = context_cache.shape[1]
    heads_width = w_v.shape[2]
    shard = w_qk.shape[1]
    allowed = jnp.concatenate(
        [jnp.repeat(tile_mask[:, 0, :1], ctx, axis=1), jnp.repeat(tile_mask[:, 0, 1:], tok, axis=1)],
        axis=1,
    )
    bias = jnp.where(allowed == 1, 0.0, -1e30).astype(jnp.float32)
    rows = LAG * ctx + MB * tok
    keys = ctx + tok
    bf, f32 = jnp.bfloat16, jnp.float32
    dma = pltpu.SemaphoreType.DMA
    anywhere = pl.BlockSpec(memory_space=pl.ANY)
    vmem = pl.BlockSpec(memory_space=pltpu.VMEM)
    out = pl.pallas_call(
        functools.partial(fused, n_dp, n_pipe),
        out_shape=jax.ShapeDtypeStruct((shard, heads_width), f32),
        in_specs=[anywhere] * 5 + [vmem, anywhere],
        out_specs=vmem,
        scratch_shapes=[
            pltpu.VMEM((width, heads_width), bf),
            pltpu.VMEM((width, heads_width), bf),
            pltpu.VMEM((width, heads_width), bf),
            pltpu.VMEM((width, heads_width), bf),
            pltpu.VMEM((rows, width), bf),
            pltpu.VMEM((MB, tok, width), bf),
            pltpu.VMEM((MB, tok, width), bf),
            pltpu.VMEM((ctx, width), bf),
            pltpu.VMEM((rows, heads_width), f32),
            pltpu.VMEM((rows, heads_width), f32),
            pltpu.VMEM((rows, heads_width), f32),
            pltpu.VMEM((tok, heads_width), bf),
            pltpu.VMEM((MB, keys, heads_width), bf),
            pltpu.VMEM((MB, keys, heads_width), bf),
            pltpu.VMEM((MB, n_dp, tok, heads_width), bf),
            pltpu.VMEM((MB, n_dp, tok, shard), bf),
            dma((LAG + MB + 5,)),
            dma((14,)),
            dma((n_dp, 2)),
            dma((MB, CHUNKS)),
            dma((MB, CHUNKS)),
            dma((n_pipe - 1, CHUNKS)),
            dma((CHUNKS,)),
            dma((MB - 1, n_dp)),
            dma((MB - 1, n_dp)),
            dma((n_dp,)),
            dma((n_dp,)),
            dma((14,)),
            dma((n_dp, 2)),
        ],
        compiler_params=pltpu.CompilerParams(
            collective_id=0, has_side_effects=True, vmem_limit_bytes=62 * 2**20
        ),
    )(latents_in, context_cache, w_qk[0], w_v[0], w_out[0], bias, out_cotangent[0])
    return out[None]


def solution(mesh):
    in_specs = (
        P(None, "dp", None),
        P(None, "dp", None),
        P("pipe", "dp", None),
        P("pipe", None, None),
        P("pipe", None, None),
        P(None, "dp", None),
        P("pipe", None, "dp", None),
    )
    out_specs = P("pipe", "dp", None)
    fits = mesh.shape["dp"] == 8 and mesh.shape["pipe"] > 1
    body = local_fused if fits else local
    return jax.shard_map(body, mesh=mesh, in_specs=in_specs, out_specs=out_specs, check_vma=False)
```

```python
import functools

import jax
import jax.numpy as jnp
import numpy as np
from jax import lax
from jax.experimental import pallas as pl
from jax.experimental.pallas import tpu as pltpu
from jax.sharding import PartitionSpec as P

HEADS = 12
HDIM = 128
TILE = 64
MB = 3
LAG = 2
PARTS = (1, 2, 3, 3, 2, 1)
CHUNKS = len(PARTS)
MESH = pl.DeviceIdType.MESH


def passed_along(block, axis, distance):
    devices = range(lax.axis_size(axis))
    route = [((i - distance) % len(devices), i) for i in devices]
    return lax.ppermute(block, axis, route)


def allowed_keys(tile_block, ctx_rows):
    columns = jnp.concatenate(
        [
            jnp.repeat(tile_block[:, :1], ctx_rows, axis=1),
            jnp.repeat(tile_block[:, 1:], TILE, axis=1),
        ],
        axis=1,
    )
    return jnp.repeat(columns, TILE, axis=0) == 1


def attend(hidden, context, tile_block, weights_q, weights_k, weights_v, weights_out):
    ctx_rows = context.shape[0]
    tok_rows = hidden.shape[0]
    heads_width = weights_v.shape[1]
    joined = jnp.concatenate([context, hidden], axis=0).astype(jnp.float32)
    normed = (joined * lax.rsqrt(jnp.mean(joined * joined, axis=-1, keepdims=True) + 1e-06)).astype(
        jnp.bfloat16
    )
    queries = jnp.dot(normed[ctx_rows:], weights_q, preferred_element_type=jnp.float32).astype(
        jnp.bfloat16
    )
    key_rows = jnp.dot(normed, weights_k, preferred_element_type=jnp.float32).astype(jnp.bfloat16)
    value_rows = jnp.dot(normed, weights_v, preferred_element_type=jnp.float32).astype(jnp.bfloat16)
    query_heads = queries.reshape(tok_rows, HEADS, HDIM)
    key_heads = key_rows.reshape(ctx_rows + tok_rows, HEADS, HDIM)
    value_heads = value_rows.reshape(ctx_rows + tok_rows, HEADS, HDIM)
    scores = jnp.einsum(
        "qhd,khd->hqk", query_heads, key_heads, preferred_element_type=jnp.float32
    ) * HDIM ** (-0.5)
    allowed = allowed_keys(tile_block, ctx_rows)
    scores = jnp.where(allowed[None], scores, -1e30)
    largest = jnp.max(scores, axis=-1, keepdims=True)
    exponent = jnp.exp(scores - largest)
    attention = (exponent / jnp.sum(exponent, axis=-1, keepdims=True)).astype(jnp.bfloat16)
    mixed_heads = jnp.einsum(
        "hqk,khd->qhd", attention, value_heads, preferred_element_type=jnp.float32
    )
    mixed_heads = mixed_heads.astype(jnp.bfloat16).reshape(tok_rows, heads_width)
    update = lax.dot_general(
        mixed_heads, weights_out, (((1,), (1,)), ((), ())), preferred_element_type=jnp.float32
    )
    result = (hidden.astype(jnp.float32) + update).astype(jnp.bfloat16)
    return (result, mixed_heads)


def local(latents_in, context_cache, w_qk, w_v, w_out, tile_mask, out_cotangent):
    segments = lax.axis_size("pipe")
    segment_index = lax.axis_index("pipe")
    tok_rows = latents_in.shape[1]
    model_width = latents_in.shape[2]
    ctx_rows = context_cache.shape[1]
    heads_width = w_v.shape[2]
    weights_q, weights_k = (
        lax.all_gather(w_qk[0][:, :heads_width], "dp", axis=0, tiled=True),
        lax.all_gather(w_qk[0][:, heads_width:], "dp", axis=0, tiled=True),
    )
    weights_v = w_v[0]
    weights_out = w_out[0]
    cotangent_local = out_cotangent[0]
    starts = [microbatch // LAG * segments + microbatch % LAG for microbatch in range(MB)]
    moments = starts[-1] + segments
    plan_table = np.full((moments, segments), -1, np.int32)
    for microbatch in range(MB):
        for section in range(segments):
            plan_table[starts[microbatch] + section, section] = microbatch
    roster = jnp.asarray(plan_table)
    records = jnp.zeros((MB, tok_rows, heads_width), jnp.bfloat16)
    incoming = jnp.zeros((tok_rows, model_width), jnp.bfloat16)
    incoming_ctx = jnp.zeros((ctx_rows, model_width), jnp.bfloat16)
    leading = segment_index == 0

    def advance(operands):
        hidden, context, chosen, kept = operands
        result, mixed_heads = attend(
            hidden, context, tile_mask[chosen], weights_q, weights_k, weights_v, weights_out
        )
        return (result, lax.dynamic_update_slice_in_dim(kept, mixed_heads[None], chosen, 0))

    def standby(operands):
        return (operands[0], operands[3])

    for moment in range(moments):
        current = roster[moment, segment_index]
        chosen = jnp.maximum(current, 0)
        hidden = jnp.where(leading, latents_in[chosen], incoming)
        first_context = jnp.where(
            chosen < LAG,
            context_cache[jnp.minimum(chosen, LAG - 1)],
            incoming[tok_rows - ctx_rows :],
        )
        context = jnp.where(leading, first_context, incoming_ctx)
        result, records = lax.cond(
            current >= 0, advance, standby, (hidden, context, chosen, records)
        )
        if moment + 1 < moments:
            incoming, incoming_ctx = passed_along((result, context), "pipe", 1)
    cotangent_rows = cotangent_local.reshape(MB * tok_rows, model_width)
    mixed_rows = records.reshape(MB * tok_rows, heads_width)
    gradient = lax.psum_scatter(
        lax.dot_general(
            cotangent_rows, mixed_rows, (((0,), (0,)), ((), ())), preferred_element_type=jnp.float32
        ).astype(jnp.bfloat16),
        "dp",
        scatter_dimension=0,
        tiled=True,
    ).astype(jnp.float32)
    return gradient[None]


def chip_neighbours(dp):
    core = dp % 2
    x = (dp // 2) % 2
    y = dp // 4
    sibling = dp + 1 - 2 * core
    along_x = y * 4 + (1 - x) * 2 + core
    along_y = (1 - y) * 4 + x * 2 + core
    across = (1 - y) * 4 + (1 - x) * 2 + core
    return sibling, along_x, along_y, across


def dot_nn(a, b):
    return jnp.dot(a, b, preferred_element_type=jnp.float32)


def dot_nt(a, b):
    return lax.dot_general(a, b, (((1,), (1,)), ((), ())), preferred_element_type=jnp.float32)


def dot_tn(a, b):
    return lax.dot_general(a, b, (((0,), (0,)), ((), ())), preferred_element_type=jnp.float32)


def row_scale(rows):
    wide = rows.astype(jnp.float32)
    return lax.rsqrt(jnp.mean(wide * wide, axis=-1, keepdims=True) + 1e-06)


def fused(
    n_dp, n_pipe, latents, cache, w_qk, w_v, w_out, mask, cot, part, o_last, ct_last,
    wq, wk, wv, wo, given, hid, outgo, ctx2, qacc, kacc, vacc, qb, kb, vb, o_all, ct_all,
    gsum,
    ld_sem, w_send, w_recv, h_send, h_recv, c_send, c_recv, o_send, o_recv, t_send, t_recv, e_send, e_recv,
):
    dp = lax.axis_index("dp")
    stage = lax.axis_index("pipe")
    sibling, along_x, along_y, across = chip_neighbours(dp)
    tok = latents.shape[1]
    ctx = cache.shape[1]
    width = latents.shape[2]
    heads_width = w_v.shape[1]
    shard = w_qk.shape[0]
    unit = width // sum(PARTS)
    edges = [unit * sum(PARTS[:c]) for c in range(CHUNKS + 1)]
    last = n_pipe - 1
    base = LAG * ctx

    loads = [
        pltpu.make_async_copy(cache.at[m], given.at[pl.ds(m * ctx, ctx)], ld_sem.at[m])
        for m in range(LAG)
    ]
    loads += [
        pltpu.make_async_copy(latents.at[m], given.at[pl.ds(base + m * tok, tok)], ld_sem.at[LAG + m])
        for m in range(MB)
    ]
    load_v = pltpu.make_async_copy(w_v, wv, ld_sem.at[LAG + MB])
    load_o = pltpu.make_async_copy(w_out, wo, ld_sem.at[LAG + MB + 1])
    own_rows = pl.ds(pl.multiple_of(dp * shard, shard), shard)
    own_q = pltpu.make_async_copy(
        w_qk.at[:, pl.ds(0, heads_width)], wq.at[own_rows], ld_sem.at[LAG + MB + 2]
    )
    own_k = pltpu.make_async_copy(
        w_qk.at[:, pl.ds(heads_width, heads_width)], wk.at[own_rows], ld_sem.at[LAG + MB + 3]
    )
    own_t = pltpu.make_async_copy(
        cot.at[:, :, pl.ds(pl.multiple_of(dp * shard, shard), shard)],
        ct_all.at[:, dp],
        ld_sem.at[LAG + MB + 4],
    )
    for copy in loads:
        copy.start()
    load_v.start()

    barrier = pltpu.get_barrier_semaphore()
    for k in range(1, n_dp):
        pl.semaphore_signal(barrier, 1, device_id=((dp + k) % n_dp, stage), device_id_type=MESH)
    for k in range(1, n_pipe):
        pl.semaphore_signal(barrier, 1, device_id=(dp, (stage + k) % n_pipe), device_id_type=MESH)
    pl.semaphore_wait(barrier, n_dp - 1 + n_pipe - 1)

    halves = (wq, wk)
    sent = []

    def rows_of(j):
        return pl.ds(pl.multiple_of(j * shard, shard), shard)

    def send_own(half, target):
        copy = pltpu.make_async_remote_copy(
            src_ref=w_qk.at[:, pl.ds(half * heads_width, heads_width)],
            dst_ref=halves[half].at[own_rows],
            send_sem=w_send.at[len(sent)],
            recv_sem=w_recv.at[dp, half],
            device_id=(target, stage),
            device_id_type=MESH,
        )
        copy.start()
        sent.append(copy)

    def piece(j, half, target, slot):
        ref = halves[half].at[rows_of(j)]
        return pltpu.make_async_remote_copy(
            src_ref=ref,
            dst_ref=ref,
            send_sem=w_send.at[slot],
            recv_sem=w_recv.at[j, half],
            device_id=(target, stage),
            device_id_type=MESH,
        )

    def forward(j, half, target):
        copy = piece(j, half, target, len(sent))
        copy.start()
        sent.append(copy)

    def arrived(j, half):
        piece(j, half, sibling, 0).wait_recv()

    send_own(0, along_y)
    send_own(1, along_x)
    send_own(1, along_y)
    send_own(0, along_x)
    send_own(0, sibling)
    send_own(1, sibling)
    own_q.start()
    own_k.start()
    load_o.start()
    own_t.start()

    for copy in loads:
        copy.wait()
    load_v.wait()
    tile = heads_width // 6

    @pl.loop(0, 6)
    def _(n):
        cols = pl.ds(pl.multiple_of(n * tile, tile), tile)
        vacc[:, cols] = dot_nn(given[...], wv[:, cols])

    qacc[...] = jnp.zeros_like(qacc)
    kacc[...] = jnp.zeros_like(kacc)

    @pl.when(stage == 0)
    def _():
        for m in range(MB):
            hid[m] = given[base + m * tok : base + (m + 1) * tok]

    wide = heads_width // 3

    def use(j, half):
        acc = (qacc, kacc)[half]
        weights = halves[half]
        first = base if half == 0 else 0

        @pl.loop(0, 3)
        def _(n):
            cols = pl.ds(pl.multiple_of(n * wide, wide), wide)
            acc[first:, cols] += dot_nn(given[first:, rows_of(j)], weights[rows_of(j), cols])

    own_q.wait()
    use(dp, 0)
    own_k.wait()
    use(dp, 1)
    arrived(sibling, 0)
    use(sibling, 0)
    arrived(sibling, 1)
    use(sibling, 1)
    arrived(along_y, 0)
    forward(along_y, 0, along_x)
    forward(along_y, 0, sibling)
    arrived(along_x, 1)
    forward(along_x, 1, along_y)
    forward(along_x, 1, sibling)
    use(along_y, 0)
    use(along_x, 1)
    arrived(along_y, 1)
    forward(along_y, 1, sibling)
    arrived(along_x, 0)
    forward(along_x, 0, sibling)
    use(along_y, 1)
    use(along_x, 0)
    sib_x, sib_y, sib_d = [
        neighbour + 1 - 2 * (dp % 2) for neighbour in (along_x, along_y, across)
    ]
    for j in (sib_y, sib_x):
        for half in range(2):
            arrived(j, half)
            use(j, half)
    for half in range(2):
        arrived(across, half)
        forward(across, half, sibling)
    for half in range(2):
        use(across, half)
    for half in range(2):
        arrived(sib_d, half)
        use(sib_d, half)

    load_o.wait()
    scale = row_scale(given[0:base])
    for m in range(LAG):
        rows = slice(m * ctx, (m + 1) * ctx)
        kb[m, 0:ctx] = (kacc[rows] * scale[rows]).astype(jnp.bfloat16)
        vb[m, 0:ctx] = (vacc[rows] * scale[rows]).astype(jnp.bfloat16)

    def hop(m, c, target):
        cols = pl.ds(edges[c], edges[c + 1] - edges[c])
        return pltpu.make_async_remote_copy(
            src_ref=outgo.at[m, :, cols],
            dst_ref=hid.at[m, :, cols],
            send_sem=h_send.at[m, c],
            recv_sem=h_recv.at[m, c],
            device_id=(dp, target),
            device_id_type=MESH,
        )

    def loop_back(c, target, slot):
        ref = ctx2.at[:, pl.ds(edges[c], edges[c + 1] - edges[c])]
        return pltpu.make_async_remote_copy(
            src_ref=ref,
            dst_ref=ref,
            send_sem=c_send.at[slot, c],
            recv_sem=c_recv.at[c],
            device_id=(dp, target),
            device_id_type=MESH,
        )

    def spread(m, k):
        target = (dp + k) % n_dp
        ref = o_all.at[m, dp]
        return pltpu.make_async_remote_copy(
            src_ref=ref,
            dst_ref=ref,
            send_sem=o_send.at[m, k],
            recv_sem=o_recv.at[m, dp],
            device_id=(target, stage),
            device_id_type=MESH,
        )

    tail_sent = []

    own_o = pltpu.make_async_copy(o_all.at[MB - 1, dp], o_last.at[dp], ld_sem.at[LAG + MB + 5])
    part_out = pltpu.make_async_copy(gsum, part, ld_sem.at[LAG + MB + 6])
    ct_out = pltpu.make_async_copy(ct_all.at[MB - 1], ct_last, ld_sem.at[LAG + MB + 7])

    def tail_piece(j, half, target, slot, own=False):
        cols = pl.ds(half * (heads_width // 2), heads_width // 2)
        ref = o_last.at[j, :, cols]
        return pltpu.make_async_remote_copy(
            src_ref=o_all.at[MB - 1, dp, :, cols] if own else ref,
            dst_ref=ref,
            send_sem=e_send.at[slot],
            recv_sem=e_recv.at[j, half],
            device_id=(target, stage),
            device_id_type=MESH,
        )

    def tail_send(j, half, target, own=False):
        copy = tail_piece(j, half, target, len(tail_sent), own)
        copy.start()
        tail_sent.append(copy)

    def tail_arrived(j, half):
        tail_piece(j, half, sibling, 0).wait_recv()

    def finish_exchange():
        tail_arrived(along_y, 0)
        tail_send(along_y, 0, along_x)
        tail_arrived(along_x, 1)
        tail_send(along_x, 1, along_y)
        tail_send(along_y, 0, sibling)
        tail_send(along_x, 1, sibling)
        tail_arrived(along_y, 1)
        tail_send(along_y, 1, sibling)
        tail_arrived(along_x, 0)
        tail_send(along_x, 0, sibling)
        for half in range(2):
            tail_arrived(across, half)
            tail_send(across, half, sibling)
        for j in (sibling, sib_y, sib_x, sib_d):
            for half in range(2):
                tail_arrived(j, half)

    def contract(rows, lhs, c, pairs):
        for acc, weights in pairs:
            term = dot_nn(lhs, weights[edges[c] : edges[c + 1], :])
            if c == 0:
                acc[rows] = term
            else:
                acc[rows] += term

    def process(m):
        rows = slice(base + m * tok, base + (m + 1) * tok)
        if m >= LAG:
            for c in range(CHUNKS):
                @pl.when(stage != last)
                def _():
                    loop_back(c, last, 0).wait_recv()

                contract(
                    slice(0, ctx), ctx2[:, edges[c] : edges[c + 1]], c, ((kacc, wk), (vacc, wv))
                )
            scale = row_scale(ctx2[...])
            kb[m, 0:ctx] = (kacc[0:ctx] * scale).astype(jnp.bfloat16)
            vb[m, 0:ctx] = (vacc[0:ctx] * scale).astype(jnp.bfloat16)

        @pl.when(stage > 0)
        def _():
            for c in range(CHUNKS):
                hop(m, c, (stage + 1) % n_pipe).wait_recv()
                contract(
                    rows,
                    hid[m, :, edges[c] : edges[c + 1]],
                    c,
                    ((qacc, wq), (kacc, wk), (vacc, wv)),
                )

        scale = row_scale(hid[m])
        qb[...] = (qacc[rows] * scale).astype(jnp.bfloat16)
        kb[m, ctx:] = (kacc[rows] * scale).astype(jnp.bfloat16)
        vb[m, ctx:] = (vacc[rows] * scale).astype(jnp.bfloat16)
        heads = [slice(h * HDIM, (h + 1) * HDIM) for h in range(HEADS)]
        scores = jnp.concatenate([dot_nt(qb[:, s], kb[m, :, s]) for s in heads], axis=0)
        in_context = lax.broadcasted_iota(jnp.int32, (1, ctx + tok), 1) < ctx
        seen = jnp.where(in_context, mask[m, 0, 0], mask[m, 0, 1]).astype(jnp.float32)
        scores = scores * HDIM ** (-0.5) + (seen - 1.0) * 1e30
        largest = jnp.max(scores, axis=-1, keepdims=True)
        exponent = jnp.exp(scores - largest)
        attention = (exponent / jnp.sum(exponent, axis=-1, keepdims=True)).astype(jnp.bfloat16)
        for h, s in enumerate(heads):
            o_all[m, dp, :, s] = dot_nn(
                attention[h * tok : (h + 1) * tok], vb[m, :, s]
            ).astype(jnp.bfloat16)
        if m == MB - 1:
            for half, target in ((0, along_y), (1, along_x), (1, along_y), (0, along_x)):
                tail_send(dp, half, target, True)
            for half in range(2):
                tail_send(dp, half, sibling, True)
            own_o.start()

        @pl.when(stage != last)
        def _():
            for c in range(CHUNKS):
                cols = slice(edges[c], edges[c + 1])
                outgo[m, :, cols] = (
                    hid[m, :, cols].astype(jnp.float32) + dot_nt(o_all[m, dp], wo[cols, :])
                ).astype(jnp.bfloat16)
                hop(m, c, (stage + 1) % n_pipe).start()

        if m + LAG < MB:
            @pl.when(stage == last)
            def _():
                for c in range(CHUNKS):
                    cols = slice(edges[c], edges[c + 1])
                    ctx2[:, cols] = (
                        hid[m, tok - ctx :, cols].astype(jnp.float32)
                        + dot_nt(o_all[m, dp, tok - ctx :, :], wo[cols, :])
                    ).astype(jnp.bfloat16)
                    loop_back(c, 0, 0).start()
                for c in range(CHUNKS):
                    loop_back(c, 0, 0).wait_send()
                for target in range(1, n_pipe - 1):
                    for c in range(CHUNKS):
                        loop_back(c, target, target).start()

        if m < MB - 1:
            for k in range(1, n_dp):
                spread(m, k).start()

    def gradient(m):
        if m == 0:
            for k in range(1, n_dp):
                source = (dp + k) % n_dp
                pltpu.make_async_remote_copy(
                    src_ref=ct_all.at[:, source],
                    dst_ref=ct_all.at[:, source],
                    send_sem=t_send.at[k],
                    recv_sem=t_recv.at[source],
                    device_id=(source, stage),
                    device_id_type=MESH,
                ).wait_recv()
        for k in range(1, n_dp):
            source = (dp + k) % n_dp
            pltpu.make_async_remote_copy(
                src_ref=o_all.at[m, source],
                dst_ref=o_all.at[m, source],
                send_sem=o_send.at[m, k],
                recv_sem=o_recv.at[m, source],
                device_id=(source, stage),
                device_id_type=MESH,
            ).wait_recv()

        left = ct_all[m].reshape(n_dp * tok, shard)

        @pl.loop(0, 3)
        def _(n):
            cols = pl.ds(pl.multiple_of(n * wide, wide), wide)
            term = dot_tn(left, o_all[m, :, :, cols].reshape(n_dp * tok, wide))
            if m == 0:
                gsum[:, cols] = term
            else:
                gsum[:, cols] += term

    process(0)
    cot_sent = []
    own_t.wait()
    for k in range(1, n_dp):
        target = (dp + k) % n_dp
        copy = pltpu.make_async_remote_copy(
            src_ref=cot.at[:, :, pl.ds(pl.multiple_of(target * shard, shard), shard)],
            dst_ref=ct_all.at[:, dp],
            send_sem=t_send.at[k],
            recv_sem=t_recv.at[dp],
            device_id=(target, stage),
            device_id_type=MESH,
        )
        copy.start()
        cot_sent.append(copy)
    for m in range(1, MB - 1):
        process(m)
    for m in range(MB - 1):
        gradient(m)
    part_out.start()
    ct_out.start()
    process(MB - 1)
    finish_exchange()
    for copy in (part_out, ct_out, own_o):
        copy.wait()

    for copy in sent + cot_sent + tail_sent:
        copy.wait_send()
    for m in range(MB - 1):
        for k in range(1, n_dp):
            spread(m, k).wait_send()

    @pl.when(stage != last)
    def _():
        for m in range(MB):
            for c in range(CHUNKS):
                hop(m, c, (stage + 1) % n_pipe).wait_send()

    @pl.when(stage == last)
    def _():
        for target in range(1, n_pipe - 1):
            for c in range(CHUNKS):
                loop_back(c, target, target).wait_send()


def local_fused(latents_in, context_cache, w_qk, w_v, w_out, tile_mask, out_cotangent):
    n_dp = lax.axis_size("dp")
    n_pipe = lax.axis_size("pipe")
    tok, width = latents_in.shape[1:]
    ctx = context_cache.shape[1]
    heads_width = w_v.shape[2]
    shard = w_qk.shape[1]
    rows = LAG * ctx + MB * tok
    keys = ctx + tok
    bf, f32 = jnp.bfloat16, jnp.float32
    dma = pltpu.SemaphoreType.DMA
    anywhere = pl.BlockSpec(memory_space=pl.ANY)
    part, o_last, ct_last = pl.pallas_call(
        functools.partial(fused, n_dp, n_pipe),
        out_shape=(
            jax.ShapeDtypeStruct((shard, heads_width), f32),
            jax.ShapeDtypeStruct((n_dp, tok, heads_width), bf),
            jax.ShapeDtypeStruct((n_dp, tok, shard), bf),
        ),
        in_specs=[anywhere] * 5 + [pl.BlockSpec(memory_space=pltpu.SMEM), anywhere],
        out_specs=(anywhere,) * 3,
        scratch_shapes=[
            pltpu.VMEM((width, heads_width), bf),
            pltpu.VMEM((width, heads_width), bf),
            pltpu.VMEM((width, heads_width), bf),
            pltpu.VMEM((width, heads_width), bf),
            pltpu.VMEM((rows, width), bf),
            pltpu.VMEM((MB, tok, width), bf),
            pltpu.VMEM((MB, tok, width), bf),
            pltpu.VMEM((ctx, width), bf),
            pltpu.VMEM((rows, heads_width), f32),
            pltpu.VMEM((rows, heads_width), f32),
            pltpu.VMEM((rows, heads_width), f32),
            pltpu.VMEM((tok, heads_width), bf),
            pltpu.VMEM((MB, keys, heads_width), bf),
            pltpu.VMEM((MB, keys, heads_width), bf),
            pltpu.VMEM((MB, n_dp, tok, heads_width), bf),
            pltpu.VMEM((MB, n_dp, tok, shard), bf),
            pltpu.VMEM((shard, heads_width), f32),
            dma((LAG + MB + 8,)),
            dma((14,)),
            dma((n_dp, 2)),
            dma((MB, CHUNKS)),
            dma((MB, CHUNKS)),
            dma((n_pipe - 1, CHUNKS)),
            dma((CHUNKS,)),
            dma((MB - 1, n_dp)),
            dma((MB - 1, n_dp)),
            dma((n_dp,)),
            dma((n_dp,)),
            dma((14,)),
            dma((n_dp, 2)),
        ],
        compiler_params=pltpu.CompilerParams(
            collective_id=0, has_side_effects=True, vmem_limit_bytes=62 * 2**20
        ),
    )(latents_in, context_cache, w_qk[0], w_v[0], w_out[0], tile_mask, out_cotangent[0])
    last_term = dot_tn(
        ct_last.reshape(n_dp * tok, shard), o_last.reshape(n_dp * tok, heads_width)
    )
    return (part + last_term)[None]


def solution(mesh):
    in_specs = (
        P(None, "dp", None),
        P(None, "dp", None),
        P("pipe", "dp", None),
        P("pipe", None, None),
        P("pipe", None, None),
        P(None, "dp", None),
        P("pipe", None, "dp", None),
    )
    out_specs = P("pipe", "dp", None)
    fits = mesh.shape["dp"] == 8 and mesh.shape["pipe"] > 1
    body = local_fused if fits else local
    return jax.shard_map(body, mesh=mesh, in_specs=in_specs, out_specs=out_specs, check_vma=False)
```

```python
import functools

import jax
import jax.numpy as jnp
import numpy as np
from jax import lax
from jax.experimental import pallas as pl
from jax.experimental.pallas import tpu as pltpu
from jax.sharding import PartitionSpec as P

HEADS = 12
HDIM = 128
TILE = 64
MB = 3
LAG = 2
PARTS = (1, 2, 3, 3, 2, 1)
CHUNKS = len(PARTS)
MESH = pl.DeviceIdType.MESH


def passed_along(block, axis, distance):
    devices = range(lax.axis_size(axis))
    route = [((i - distance) % len(devices), i) for i in devices]
    return lax.ppermute(block, axis, route)


def allowed_keys(tile_block, ctx_rows):
    columns = jnp.concatenate(
        [
            jnp.repeat(tile_block[:, :1], ctx_rows, axis=1),
            jnp.repeat(tile_block[:, 1:], TILE, axis=1),
        ],
        axis=1,
    )
    return jnp.repeat(columns, TILE, axis=0) == 1


def attend(hidden, context, tile_block, weights_q, weights_k, weights_v, weights_out):
    ctx_rows = context.shape[0]
    tok_rows = hidden.shape[0]
    heads_width = weights_v.shape[1]
    joined = jnp.concatenate([context, hidden], axis=0).astype(jnp.float32)
    normed = (joined * lax.rsqrt(jnp.mean(joined * joined, axis=-1, keepdims=True) + 1e-06)).astype(
        jnp.bfloat16
    )
    queries = jnp.dot(normed[ctx_rows:], weights_q, preferred_element_type=jnp.float32).astype(
        jnp.bfloat16
    )
    key_rows = jnp.dot(normed, weights_k, preferred_element_type=jnp.float32).astype(jnp.bfloat16)
    value_rows = jnp.dot(normed, weights_v, preferred_element_type=jnp.float32).astype(jnp.bfloat16)
    query_heads = queries.reshape(tok_rows, HEADS, HDIM)
    key_heads = key_rows.reshape(ctx_rows + tok_rows, HEADS, HDIM)
    value_heads = value_rows.reshape(ctx_rows + tok_rows, HEADS, HDIM)
    scores = jnp.einsum(
        "qhd,khd->hqk", query_heads, key_heads, preferred_element_type=jnp.float32
    ) * HDIM ** (-0.5)
    allowed = allowed_keys(tile_block, ctx_rows)
    scores = jnp.where(allowed[None], scores, -1e30)
    largest = jnp.max(scores, axis=-1, keepdims=True)
    exponent = jnp.exp(scores - largest)
    attention = (exponent / jnp.sum(exponent, axis=-1, keepdims=True)).astype(jnp.bfloat16)
    mixed_heads = jnp.einsum(
        "hqk,khd->qhd", attention, value_heads, preferred_element_type=jnp.float32
    )
    mixed_heads = mixed_heads.astype(jnp.bfloat16).reshape(tok_rows, heads_width)
    update = lax.dot_general(
        mixed_heads, weights_out, (((1,), (1,)), ((), ())), preferred_element_type=jnp.float32
    )
    result = (hidden.astype(jnp.float32) + update).astype(jnp.bfloat16)
    return (result, mixed_heads)


def local(latents_in, context_cache, w_qk, w_v, w_out, tile_mask, out_cotangent):
    segments = lax.axis_size("pipe")
    segment_index = lax.axis_index("pipe")
    tok_rows = latents_in.shape[1]
    model_width = latents_in.shape[2]
    ctx_rows = context_cache.shape[1]
    heads_width = w_v.shape[2]
    weights_q, weights_k = (
        lax.all_gather(w_qk[0][:, :heads_width], "dp", axis=0, tiled=True),
        lax.all_gather(w_qk[0][:, heads_width:], "dp", axis=0, tiled=True),
    )
    weights_v = w_v[0]
    weights_out = w_out[0]
    cotangent_local = out_cotangent[0]
    starts = [microbatch // LAG * segments + microbatch % LAG for microbatch in range(MB)]
    moments = starts[-1] + segments
    plan_table = np.full((moments, segments), -1, np.int32)
    for microbatch in range(MB):
        for section in range(segments):
            plan_table[starts[microbatch] + section, section] = microbatch
    roster = jnp.asarray(plan_table)
    records = jnp.zeros((MB, tok_rows, heads_width), jnp.bfloat16)
    incoming = jnp.zeros((tok_rows, model_width), jnp.bfloat16)
    incoming_ctx = jnp.zeros((ctx_rows, model_width), jnp.bfloat16)
    leading = segment_index == 0

    def advance(operands):
        hidden, context, chosen, kept = operands
        result, mixed_heads = attend(
            hidden, context, tile_mask[chosen], weights_q, weights_k, weights_v, weights_out
        )
        return (result, lax.dynamic_update_slice_in_dim(kept, mixed_heads[None], chosen, 0))

    def standby(operands):
        return (operands[0], operands[3])

    for moment in range(moments):
        current = roster[moment, segment_index]
        chosen = jnp.maximum(current, 0)
        hidden = jnp.where(leading, latents_in[chosen], incoming)
        first_context = jnp.where(
            chosen < LAG,
            context_cache[jnp.minimum(chosen, LAG - 1)],
            incoming[tok_rows - ctx_rows :],
        )
        context = jnp.where(leading, first_context, incoming_ctx)
        result, records = lax.cond(
            current >= 0, advance, standby, (hidden, context, chosen, records)
        )
        if moment + 1 < moments:
            incoming, incoming_ctx = passed_along((result, context), "pipe", 1)
    cotangent_rows = cotangent_local.reshape(MB * tok_rows, model_width)
    mixed_rows = records.reshape(MB * tok_rows, heads_width)
    gradient = lax.psum_scatter(
        lax.dot_general(
            cotangent_rows, mixed_rows, (((0,), (0,)), ((), ())), preferred_element_type=jnp.float32
        ).astype(jnp.bfloat16),
        "dp",
        scatter_dimension=0,
        tiled=True,
    ).astype(jnp.float32)
    return gradient[None]


def chip_neighbours(dp):
    core = dp % 2
    x = (dp // 2) % 2
    y = dp // 4
    sibling = dp + 1 - 2 * core
    along_x = y * 4 + (1 - x) * 2 + core
    along_y = (1 - y) * 4 + x * 2 + core
    across = (1 - y) * 4 + (1 - x) * 2 + core
    return sibling, along_x, along_y, across


def dot_nn(a, b):
    return jnp.dot(a, b, preferred_element_type=jnp.float32)


def dot_nt(a, b):
    return lax.dot_general(a, b, (((1,), (1,)), ((), ())), preferred_element_type=jnp.float32)


def dot_tn(a, b):
    return lax.dot_general(a, b, (((0,), (0,)), ((), ())), preferred_element_type=jnp.float32)


def row_scale(rows):
    wide = rows.astype(jnp.float32)
    return lax.rsqrt(jnp.mean(wide * wide, axis=-1, keepdims=True) + 1e-06)


def fused(
    n_dp, n_pipe, latents, cache, w_qk, w_v, w_out, mask, cot, part, o_last, ct_last,
    wq, wk, wv, wo, given, hid, outgo, ctx2, qacc, kacc, vacc, qb, kb, vb, o_all, ct_all,
    gsum,
    ld_sem, w_send, w_recv, h_send, h_recv, c_send, c_recv, o_send, o_recv, t_send, t_recv, e_send, e_recv,
):
    dp = lax.axis_index("dp")
    stage = lax.axis_index("pipe")
    sibling, along_x, along_y, across = chip_neighbours(dp)
    tok = latents.shape[1]
    ctx = cache.shape[1]
    width = latents.shape[2]
    heads_width = w_v.shape[1]
    shard = w_qk.shape[0]
    unit = width // sum(PARTS)
    edges = [unit * sum(PARTS[:c]) for c in range(CHUNKS + 1)]
    last = n_pipe - 1
    base = LAG * ctx

    loads = [
        pltpu.make_async_copy(cache.at[m], given.at[pl.ds(m * ctx, ctx)], ld_sem.at[m])
        for m in range(LAG)
    ]
    loads += [
        pltpu.make_async_copy(latents.at[m], given.at[pl.ds(base + m * tok, tok)], ld_sem.at[LAG + m])
        for m in range(MB)
    ]
    load_v = pltpu.make_async_copy(w_v, wv, ld_sem.at[LAG + MB])
    load_o = pltpu.make_async_copy(w_out, wo, ld_sem.at[LAG + MB + 1])
    own_rows = pl.ds(pl.multiple_of(dp * shard, shard), shard)
    own_q = pltpu.make_async_copy(
        w_qk.at[:, pl.ds(0, heads_width)], wq.at[own_rows], ld_sem.at[LAG + MB + 2]
    )
    own_k = pltpu.make_async_copy(
        w_qk.at[:, pl.ds(heads_width, heads_width)], wk.at[own_rows], ld_sem.at[LAG + MB + 3]
    )
    own_t = pltpu.make_async_copy(
        cot.at[:, :, pl.ds(pl.multiple_of(dp * shard, shard), shard)],
        ct_all.at[:, dp],
        ld_sem.at[LAG + MB + 4],
    )
    for copy in loads:
        copy.start()
    load_v.start()

    barrier = pltpu.get_barrier_semaphore()
    for k in range(1, n_dp):
        pl.semaphore_signal(barrier, 1, device_id=((dp + k) % n_dp, stage), device_id_type=MESH)
    for k in range(1, n_pipe):
        pl.semaphore_signal(barrier, 1, device_id=(dp, (stage + k) % n_pipe), device_id_type=MESH)
    pl.semaphore_wait(barrier, n_dp - 1 + n_pipe - 1)

    halves = (wq, wk)
    sent = []

    def rows_of(j):
        return pl.ds(pl.multiple_of(j * shard, shard), shard)

    def send_own(half, target):
        copy = pltpu.make_async_remote_copy(
            src_ref=w_qk.at[:, pl.ds(half * heads_width, heads_width)],
            dst_ref=halves[half].at[own_rows],
            send_sem=w_send.at[len(sent)],
            recv_sem=w_recv.at[dp, half],
            device_id=(target, stage),
            device_id_type=MESH,
        )
        copy.start()
        sent.append(copy)

    def piece(j, half, target, slot):
        ref = halves[half].at[rows_of(j)]
        return pltpu.make_async_remote_copy(
            src_ref=ref,
            dst_ref=ref,
            send_sem=w_send.at[slot],
            recv_sem=w_recv.at[j, half],
            device_id=(target, stage),
            device_id_type=MESH,
        )

    def forward(j, half, target):
        copy = piece(j, half, target, len(sent))
        copy.start()
        sent.append(copy)

    def arrived(j, half):
        piece(j, half, sibling, 0).wait_recv()

    send_own(0, along_y)
    send_own(1, along_x)
    send_own(1, along_y)
    send_own(0, along_x)
    send_own(0, sibling)
    send_own(1, sibling)
    own_q.start()
    own_k.start()
    load_o.start()
    own_t.start()

    for copy in loads:
        copy.wait()
    load_v.wait()
    tile = heads_width // 6

    @pl.loop(0, 6)
    def _(n):
        cols = pl.ds(pl.multiple_of(n * tile, tile), tile)
        vacc[:, cols] = dot_nn(given[...], wv[:, cols])

    qacc[...] = jnp.zeros_like(qacc)
    kacc[...] = jnp.zeros_like(kacc)

    @pl.when(stage == 0)
    def _():
        for m in range(MB):
            hid[m] = given[base + m * tok : base + (m + 1) * tok]

    wide = heads_width // 3

    def use(j, half):
        acc = (qacc, kacc)[half]
        weights = halves[half]
        first = base if half == 0 else 0

        @pl.loop(0, 3)
        def _(n):
            cols = pl.ds(pl.multiple_of(n * wide, wide), wide)
            acc[first:, cols] += dot_nn(given[first:, rows_of(j)], weights[rows_of(j), cols])

    own_q.wait()
    use(dp, 0)
    own_k.wait()
    use(dp, 1)
    arrived(sibling, 0)
    use(sibling, 0)
    arrived(sibling, 1)
    use(sibling, 1)
    arrived(along_y, 0)
    forward(along_y, 0, along_x)
    forward(along_y, 0, sibling)
    arrived(along_x, 1)
    forward(along_x, 1, along_y)
    forward(along_x, 1, sibling)
    use(along_y, 0)
    use(along_x, 1)
    arrived(along_y, 1)
    forward(along_y, 1, sibling)
    arrived(along_x, 0)
    forward(along_x, 0, sibling)
    use(along_y, 1)
    use(along_x, 0)
    sib_x, sib_y, sib_d = [
        neighbour + 1 - 2 * (dp % 2) for neighbour in (along_x, along_y, across)
    ]
    for j in (sib_y, sib_x):
        for half in range(2):
            arrived(j, half)
            use(j, half)
    for half in range(2):
        arrived(across, half)
        forward(across, half, sibling)
    for half in range(2):
        use(across, half)
    for half in range(2):
        arrived(sib_d, half)
        use(sib_d, half)

    load_o.wait()
    scale = row_scale(given[0:base])
    for m in range(LAG):
        rows = slice(m * ctx, (m + 1) * ctx)
        kb[m, 0:ctx] = (kacc[rows] * scale[rows]).astype(jnp.bfloat16)
        vb[m, 0:ctx] = (vacc[rows] * scale[rows]).astype(jnp.bfloat16)

    def hop(m, c, target):
        cols = pl.ds(edges[c], edges[c + 1] - edges[c])
        return pltpu.make_async_remote_copy(
            src_ref=outgo.at[m, :, cols],
            dst_ref=hid.at[m, :, cols],
            send_sem=h_send.at[m, c],
            recv_sem=h_recv.at[m, c],
            device_id=(dp, target),
            device_id_type=MESH,
        )

    def loop_back(c, target, slot):
        ref = ctx2.at[:, pl.ds(edges[c], edges[c + 1] - edges[c])]
        return pltpu.make_async_remote_copy(
            src_ref=ref,
            dst_ref=ref,
            send_sem=c_send.at[slot, c],
            recv_sem=c_recv.at[c],
            device_id=(dp, target),
            device_id_type=MESH,
        )

    def spread(m, k):
        target = (dp + k) % n_dp
        ref = o_all.at[m, dp]
        return pltpu.make_async_remote_copy(
            src_ref=ref,
            dst_ref=ref,
            send_sem=o_send.at[m, k],
            recv_sem=o_recv.at[m, dp],
            device_id=(target, stage),
            device_id_type=MESH,
        )

    tail_sent = []

    own_o = pltpu.make_async_copy(o_all.at[MB - 1, dp], o_last.at[dp], ld_sem.at[LAG + MB + 5])
    part_out = pltpu.make_async_copy(gsum, part, ld_sem.at[LAG + MB + 6])
    ct_out = pltpu.make_async_copy(ct_all.at[MB - 1], ct_last, ld_sem.at[LAG + MB + 7])

    def tail_piece(j, half, target, slot, own=False):
        cols = pl.ds(half * (heads_width // 2), heads_width // 2)
        ref = o_last.at[j, :, cols]
        return pltpu.make_async_remote_copy(
            src_ref=o_all.at[MB - 1, dp, :, cols] if own else ref,
            dst_ref=ref,
            send_sem=e_send.at[slot],
            recv_sem=e_recv.at[j, half],
            device_id=(target, stage),
            device_id_type=MESH,
        )

    def tail_send(j, half, target, own=False):
        copy = tail_piece(j, half, target, len(tail_sent), own)
        copy.start()
        tail_sent.append(copy)

    def tail_arrived(j, half):
        tail_piece(j, half, sibling, 0).wait_recv()

    def finish_exchange():
        tail_arrived(along_y, 0)
        tail_send(along_y, 0, along_x)
        tail_arrived(along_x, 1)
        tail_send(along_x, 1, along_y)
        tail_send(along_y, 0, sibling)
        tail_send(along_x, 1, sibling)
        tail_arrived(along_y, 1)
        tail_send(along_y, 1, sibling)
        tail_arrived(along_x, 0)
        tail_send(along_x, 0, sibling)
        for half in range(2):
            tail_arrived(across, half)
            tail_send(across, half, sibling)
        for j in (sibling, sib_y, sib_x, sib_d):
            for half in range(2):
                tail_arrived(j, half)

    def contract(rows, lhs, c, pairs):
        for acc, weights in pairs:
            term = dot_nn(lhs, weights[edges[c] : edges[c + 1], :])
            if c == 0:
                acc[rows] = term
            else:
                acc[rows] += term

    def process(m):
        rows = slice(base + m * tok, base + (m + 1) * tok)
        if m >= LAG:
            for c in range(CHUNKS):
                @pl.when(stage != last)
                def _():
                    loop_back(c, last, 0).wait_recv()

                contract(
                    slice(0, ctx), ctx2[:, edges[c] : edges[c + 1]], c, ((kacc, wk), (vacc, wv))
                )
            scale = row_scale(ctx2[...])
            kb[m, 0:ctx] = (kacc[0:ctx] * scale).astype(jnp.bfloat16)
            vb[m, 0:ctx] = (vacc[0:ctx] * scale).astype(jnp.bfloat16)

        @pl.when(stage > 0)
        def _():
            for c in range(CHUNKS):
                hop(m, c, (stage + 1) % n_pipe).wait_recv()
                contract(
                    rows,
                    hid[m, :, edges[c] : edges[c + 1]],
                    c,
                    ((qacc, wq), (kacc, wk), (vacc, wv)),
                )

        scale = row_scale(hid[m])
        qb[...] = (qacc[rows] * scale).astype(jnp.bfloat16)
        kb[m, ctx:] = (kacc[rows] * scale).astype(jnp.bfloat16)
        vb[m, ctx:] = (vacc[rows] * scale).astype(jnp.bfloat16)
        heads = [slice(h * HDIM, (h + 1) * HDIM) for h in range(HEADS)]
        scores = jnp.concatenate([dot_nt(qb[:, s], kb[m, :, s]) for s in heads], axis=0)
        in_context = lax.broadcasted_iota(jnp.int32, (1, ctx + tok), 1) < ctx
        seen = jnp.where(in_context, mask[m, 0, 0], mask[m, 0, 1]).astype(jnp.float32)
        scores = scores * HDIM ** (-0.5) + (seen - 1.0) * 1e30
        largest = jnp.max(scores, axis=-1, keepdims=True)
        exponent = jnp.exp(scores - largest)
        attention = (exponent / jnp.sum(exponent, axis=-1, keepdims=True)).astype(jnp.bfloat16)
        for h, s in enumerate(heads):
            o_all[m, dp, :, s] = dot_nn(
                attention[h * tok : (h + 1) * tok], vb[m, :, s]
            ).astype(jnp.bfloat16)
        @pl.when(stage != last)
        def _():
            for c in range(CHUNKS):
                cols = slice(edges[c], edges[c + 1])
                outgo[m, :, cols] = (
                    hid[m, :, cols].astype(jnp.float32) + dot_nt(o_all[m, dp], wo[cols, :])
                ).astype(jnp.bfloat16)
                hop(m, c, (stage + 1) % n_pipe).start()

        if m + LAG < MB:
            @pl.when(stage == last)
            def _():
                for c in range(CHUNKS):
                    cols = slice(edges[c], edges[c + 1])
                    ctx2[:, cols] = (
                        hid[m, tok - ctx :, cols].astype(jnp.float32)
                        + dot_nt(o_all[m, dp, tok - ctx :, :], wo[cols, :])
                    ).astype(jnp.bfloat16)
                    loop_back(c, 0, 0).start()
                for c in range(CHUNKS):
                    loop_back(c, 0, 0).wait_send()
                for target in range(1, n_pipe - 1):
                    for c in range(CHUNKS):
                        loop_back(c, target, target).start()

        if m < MB - 1:
            for k in range(1, n_dp):
                spread(m, k).start()

        if m == MB - 1:
            for half, target in ((0, along_y), (1, along_x), (1, along_y), (0, along_x)):
                tail_send(dp, half, target, True)
            for half in range(2):
                tail_send(dp, half, sibling, True)
            own_o.start()

    def gradient(m):
        if m == 0:
            for k in range(1, n_dp):
                source = (dp + k) % n_dp
                pltpu.make_async_remote_copy(
                    src_ref=ct_all.at[:, source],
                    dst_ref=ct_all.at[:, source],
                    send_sem=t_send.at[k],
                    recv_sem=t_recv.at[source],
                    device_id=(source, stage),
                    device_id_type=MESH,
                ).wait_recv()
        for k in range(1, n_dp):
            source = (dp + k) % n_dp
            pltpu.make_async_remote_copy(
                src_ref=o_all.at[m, source],
                dst_ref=o_all.at[m, source],
                send_sem=o_send.at[m, k],
                recv_sem=o_recv.at[m, source],
                device_id=(source, stage),
                device_id_type=MESH,
            ).wait_recv()

        left = ct_all[m].reshape(n_dp * tok, shard)

        @pl.loop(0, 3)
        def _(n):
            cols = pl.ds(pl.multiple_of(n * wide, wide), wide)
            term = dot_tn(left, o_all[m, :, :, cols].reshape(n_dp * tok, wide))
            if m == 0:
                gsum[:, cols] = term
            else:
                gsum[:, cols] += term

    process(0)
    cot_sent = []
    own_t.wait()
    for k in range(1, n_dp):
        target = (dp + k) % n_dp
        copy = pltpu.make_async_remote_copy(
            src_ref=cot.at[:, :, pl.ds(pl.multiple_of(target * shard, shard), shard)],
            dst_ref=ct_all.at[:, dp],
            send_sem=t_send.at[k],
            recv_sem=t_recv.at[dp],
            device_id=(target, stage),
            device_id_type=MESH,
        )
        copy.start()
        cot_sent.append(copy)
    for m in range(1, MB - 1):
        process(m)
    for m in range(MB - 1):
        gradient(m)
    part_out.start()
    ct_out.start()
    process(MB - 1)
    finish_exchange()
    for copy in (part_out, ct_out, own_o):
        copy.wait()

    for copy in sent + cot_sent + tail_sent:
        copy.wait_send()
    for m in range(MB - 1):
        for k in range(1, n_dp):
            spread(m, k).wait_send()

    @pl.when(stage != last)
    def _():
        for m in range(MB):
            for c in range(CHUNKS):
                hop(m, c, (stage + 1) % n_pipe).wait_send()

    @pl.when(stage == last)
    def _():
        for target in range(1, n_pipe - 1):
            for c in range(CHUNKS):
                loop_back(c, target, target).wait_send()


def local_fused(latents_in, context_cache, w_qk, w_v, w_out, tile_mask, out_cotangent):
    n_dp = lax.axis_size("dp")
    n_pipe = lax.axis_size("pipe")
    tok, width = latents_in.shape[1:]
    ctx = context_cache.shape[1]
    heads_width = w_v.shape[2]
    shard = w_qk.shape[1]
    rows = LAG * ctx + MB * tok
    keys = ctx + tok
    bf, f32 = jnp.bfloat16, jnp.float32
    dma = pltpu.SemaphoreType.DMA
    anywhere = pl.BlockSpec(memory_space=pl.ANY)
    part, o_last, ct_last = pl.pallas_call(
        functools.partial(fused, n_dp, n_pipe),
        out_shape=(
            jax.ShapeDtypeStruct((shard, heads_width), f32),
            jax.ShapeDtypeStruct((n_dp, tok, heads_width), bf),
            jax.ShapeDtypeStruct((n_dp, tok, shard), bf),
        ),
        in_specs=[anywhere] * 5 + [pl.BlockSpec(memory_space=pltpu.SMEM), anywhere],
        out_specs=(anywhere,) * 3,
        scratch_shapes=[
            pltpu.VMEM((width, heads_width), bf),
            pltpu.VMEM((width, heads_width), bf),
            pltpu.VMEM((width, heads_width), bf),
            pltpu.VMEM((width, heads_width), bf),
            pltpu.VMEM((rows, width), bf),
            pltpu.VMEM((MB, tok, width), bf),
            pltpu.VMEM((MB, tok, width), bf),
            pltpu.VMEM((ctx, width), bf),
            pltpu.VMEM((rows, heads_width), f32),
            pltpu.VMEM((rows, heads_width), f32),
            pltpu.VMEM((rows, heads_width), f32),
            pltpu.VMEM((tok, heads_width), bf),
            pltpu.VMEM((MB, keys, heads_width), bf),
            pltpu.VMEM((MB, keys, heads_width), bf),
            pltpu.VMEM((MB, n_dp, tok, heads_width), bf),
            pltpu.VMEM((MB, n_dp, tok, shard), bf),
            pltpu.VMEM((shard, heads_width), f32),
            dma((LAG + MB + 8,)),
            dma((14,)),
            dma((n_dp, 2)),
            dma((MB, CHUNKS)),
            dma((MB, CHUNKS)),
            dma((n_pipe - 1, CHUNKS)),
            dma((CHUNKS,)),
            dma((MB - 1, n_dp)),
            dma((MB - 1, n_dp)),
            dma((n_dp,)),
            dma((n_dp,)),
            dma((14,)),
            dma((n_dp, 2)),
        ],
        compiler_params=pltpu.CompilerParams(
            collective_id=0, has_side_effects=True, vmem_limit_bytes=62 * 2**20
        ),
    )(latents_in, context_cache, w_qk[0], w_v[0], w_out[0], tile_mask, out_cotangent[0])
    last_term = dot_tn(
        ct_last.reshape(n_dp * tok, shard), o_last.reshape(n_dp * tok, heads_width)
    )
    return (part + last_term)[None]


def solution(mesh):
    in_specs = (
        P(None, "dp", None),
        P(None, "dp", None),
        P("pipe", "dp", None),
        P("pipe", None, None),
        P("pipe", None, None),
        P(None, "dp", None),
        P("pipe", None, "dp", None),
    )
    out_specs = P("pipe", "dp", None)
    fits = mesh.shape["dp"] == 8 and mesh.shape["pipe"] > 1
    body = local_fused if fits else local
    return jax.shard_map(body, mesh=mesh, in_specs=in_specs, out_specs=out_specs, check_vma=False)
```
